32 devices in a mesh: groups: 1, ep: 32 (over z, y, x, core).
Axes of the slice: x: 2, y: 2, z: 4, core: 2. Of those that a mesh axis runs over, the one named last changes fastest.
Arguments:
- hidden_rows: bfloat16 [256, 7168], P(('groups', 'ep')), may hold values from -6 to 6
- expert_ids: int32 [256, 2], P(('groups', 'ep')), may hold values from 0 to 3, all different within a row; in each aligned block of 8 rows (0 to 7, 8 to 15, ...) at most 8 rows name the same one
- gate_weights: float32 [256, 2], P(('groups', 'ep')), may hold values from 0.2 to 1
- w_gate: bfloat16 [7168, 8192], P(None, 'ep'), may hold values from -0.0625 to 0.0625
- w_up: bfloat16 [7168, 8192], P(None, 'ep'), may hold values from -0.0625 to 0.0625
- w_down: bfloat16 [8192, 7168], P('ep'), may hold values from -0.125 to 0.125
- latent_cache: bfloat16 [256, 48, 576], P(('groups', 'ep')), may hold values from -6 to 6
- new_latent: bfloat16 [256, 576], P(('groups', 'ep')), may hold values from -6 to 6
- parents: int32 [256, 1], P(('groups', 'ep')), may hold values from 0 to 7; in each aligned block of 8 rows (0 to 7, 8 to 15, ...) at most 2 rows name the same one
- lengths: int32 [256], P(('groups', 'ep')), may hold values from 1 to 47
Outputs:
- moe_out: bfloat16 [256, 7168], P(('groups', 'ep'))
- new_cache: bfloat16 [256, 48, 576], P(('groups', 'ep'))
The draws below stay inside these ranges and needn't reach their ends.
Inputs may be any that keep to these rules, and one draw needn't show every extreme that they name: `parents`: among the rows of one device (aligned blocks of 8 rows) no parent beam is named more than 2 times; in some blocks one is named exactly 2 times. `expert_ids`: each row names 2 different experts; among the rows of one device (aligned blocks of 8 rows) no expert is named more than 8 times, and in some blocks one is named exactly 8 times.
All inputs are finite; a program needn't handle non-finite values.
Results may differ from the reference program's by a relative error of at most 0.0064.
Values may be sent and summed in bfloat16 or wider, within the bound.
No kernel may reach another device: no remote copies, remote signals or barrier semaphores. Data moves between devices by JAX's collectives and lax.ppermute only.
A program may use at most 64 MiB of HBM per device.

```python
import math
import jax
import jax.numpy as jnp
import numpy as np
from jax import lax

D = 7168
FF = 2048
HID_DEV = 256
LAT = 576
SUF = 48
TOP = 2
BEAMS = 8
ROWS_DEV = 8
SPLIT = 8
EXPERTS = 4
CAP = 2
ECAP = 8
REQUESTS = 32
ROWS = 256
N_EP = 32


def touch_ends(drawn, rng, low, top_value):
    longest = drawn.shape.index(max(drawn.shape))
    spots = []
    for shift in (0, 1):
        where = [jax.random.randint(jax.random.fold_in(rng, axis), (), 0, length) for axis, length in enumerate(drawn.shape)]
        where[longest] = (where[longest] + shift) % drawn.shape[longest]
        spots.append(tuple(where))
    return drawn.at[spots[0]].set(low).at[spots[1]].set(top_value)


def steps_of(key, dims, pieces, least, top_value):
    loudness = 1.0
    for dim, shards_of in pieces:
        draws = jax.random.uniform(jax.random.fold_in(jax.random.fold_in(key, 6), dim), (shards_of,), jnp.float32, least / len(pieces), top_value / len(pieces))
        loudness = loudness * jnp.repeat(jnp.exp(draws), dims[dim] // shards_of).reshape((-1,) + (1,) * (len(dims) - 1 - dim))
    return loudness


def assign_block(key, own, number, rows, amount, top, limit, lean):
    order = jax.random.permutation(key, amount)
    heavy_load, usual = load_shares(amount, rows * top, limit, lean, True), load_shares(amount, rows * top, limit, lean, False)
    places = jnp.arange(amount)

    def named(sizes, rotation):
        used = int((sizes > 0).sum())
        fixed = max(1, used // 4)
        moved = fixed + (places - fixed + rotation * (used - fixed)) % max(1, amount - fixed)
        return jnp.zeros((amount,), jnp.int32).at[order[jnp.where(places < fixed, places, moved)]].set(jnp.asarray(sizes, jnp.int32))

    sizes = jnp.where(number % 4 == 0, named(heavy_load, number // 4), named(usual, number - number // 4 - 1))
    mixed = jax.random.permutation(jax.random.fold_in(own, 3), amount)
    source_of, receiver = mixed[0:amount // 2 * 2:2], mixed[1:amount // 2 * 2:2]
    margin = jnp.minimum(sizes[source_of] - 1, limit - sizes[receiver]) // 2
    margin = jnp.where((source_of == order[0]) | (receiver == order[0]) | (sizes[receiver] == 0), 0, jnp.maximum(margin, 0))
    moved = jax.random.randint(jax.random.fold_in(own, 4), (amount // 2,), 0, 1 << 20) % (margin + 1)
    sizes = sizes.at[source_of].add(-moved).at[receiver].add(moved)
    items = jnp.searchsorted(jnp.cumsum(sizes), jnp.arange(rows * top), side="right").astype(jnp.int32)
    listing = items.reshape(top, rows).T
    listing = listing[jax.random.permutation(jax.random.fold_in(own, 1), rows)]
    rotation = jax.random.randint(jax.random.fold_in(own, 2), (rows, 1), 0, top)
    return jnp.take_along_axis(listing, (jnp.arange(top)[None, :] + rotation) % top, axis=1)


def load_shares(count, total, limit, lean, full):
    portions = [(1 << 20) // math.isqrt(grade ** lean) + 1 for grade in range(1, count + 1)]
    largest = limit if full else min(limit, max(-(-total // count), total * portions[0] // sum(portions)))
    least = 1 if total - largest >= count - 1 else 0
    holding, spare = [largest] + [least] * (count - 1), total - largest - least * (count - 1)
    while spare > 0:
        free = [i for i in range(1, count) if holding[i] < largest] or [i for i in range(1, count) if holding[i] < limit]
        mass, budget = sum([portions[i] for i in free]), spare
        for i in free:
            more = min(limit - holding[i], max(1, budget * portions[i] // mass), spare)
            holding[i] = holding[i] + more
            spare = spare - more
    return np.array(holding)


def centred(key, shape, width, bound, shards=(), kind=jnp.bfloat16):
    array = width * jax.random.normal(key, shape, jnp.float32)
    if shards:
        array = array * steps_of(key, shape, shards, -0.22, 0.18)
    return jnp.clip(array, -bound, bound).astype(kind)


def setup_inputs(seed: int = 0, part: int = 0) -> dict:
    keys = jax.random.split(jax.random.key(seed), 11)
    part_keys = jax.random.split(jax.random.fold_in(keys[10], part), 11)
    hidden_rows = centred(part_keys[0], (ROWS, D), 1.0, 6.0, ((0, 32),))
    expert_ids_keys = jax.random.split(jax.random.fold_in(part_keys[1], 1), ROWS // ROWS_DEV)
    expert_ids_turns = jax.random.permutation(jax.random.fold_in(part_keys[1], 3), ROWS // ROWS_DEV)
    expert_ids = jax.vmap(lambda own, number: assign_block(jax.random.fold_in(part_keys[1], 2), own, number, ROWS_DEV, EXPERTS, TOP, ECAP, 2))(expert_ids_keys, expert_ids_turns).reshape((ROWS, TOP))
    gate_weights = jnp.clip(0.2 + 0.8 * jax.random.uniform(part_keys[2], (ROWS, TOP), jnp.float32) ** steps_of(part_keys[2], (ROWS, TOP), ((0, 32),), -0.2, 0.2), 0.2, 1.0)
    w_gate = centred(keys[3], (D, EXPERTS * FF), D ** -0.5, 0.0625, ((1, 32),))
    w_up = centred(keys[4], (D, EXPERTS * FF), D ** -0.5, 0.0625, ((1, 32),))
    w_down = centred(keys[5], (EXPERTS * FF, D), FF ** -0.5, 0.125, ((0, 32),))
    latent_cache = centred(part_keys[6], (ROWS, SUF, LAT), 1.0, 6.0, ((0, 32),))
    new_latent = centred(part_keys[7], (ROWS, LAT), 1.0, 6.0, ((0, 32),))
    parents_keys = jax.random.split(jax.random.fold_in(part_keys[8], 1), ROWS // ROWS_DEV)
    parents_turns = jax.random.permutation(jax.random.fold_in(part_keys[8], 3), ROWS // ROWS_DEV)
    parents = jax.vmap(lambda own, number: assign_block(jax.random.fold_in(part_keys[8], 2), own, number, ROWS_DEV, BEAMS, 1, CAP, 2))(parents_keys, parents_turns).reshape((ROWS, 1))
    lengths = touch_ends(jax.random.randint(part_keys[9], (ROWS,), 1, SUF), jax.random.fold_in(part_keys[9], 1), 1, SUF - 1).astype(jnp.int32)
    return dict(hidden_rows=hidden_rows, expert_ids=expert_ids, gate_weights=gate_weights, w_gate=w_gate, w_up=w_up, w_down=w_down, latent_cache=latent_cache, new_latent=new_latent, parents=parents, lengths=lengths)


def slot_table(expert_ids):
    blocks = expert_ids.reshape(N_EP, ROWS_DEV, TOP)
    chosen = (blocks[:, :, :, None] == jnp.arange(EXPERTS, dtype=jnp.int32)[None, None, None, :]).astype(jnp.int32)
    hit_count = jnp.sum(chosen, axis=2)
    before = jnp.cumsum(hit_count, axis=1) - hit_count
    position = jnp.take_along_axis(before, blocks, axis=2)
    source = jnp.arange(N_EP, dtype=jnp.int32)[:, None, None]
    return (source * ECAP + position).reshape(ROWS, TOP).astype(jnp.int32)


def reference(hidden_rows, expert_ids, gate_weights, w_gate, w_up, w_down, latent_cache, new_latent, parents, lengths):
    row_ids = jnp.arange(ROWS, dtype=jnp.int32)
    slot_of = slot_table(expert_ids)
    slot_rows = jnp.full((EXPERTS, N_EP * ECAP), ROWS, dtype=jnp.int32)
    slot_rows = slot_rows.at[expert_ids, slot_of].set(jnp.broadcast_to(row_ids[:, None], (ROWS, TOP)))
    padded = jnp.concatenate([hidden_rows, jnp.zeros((1, D), hidden_rows.dtype)], axis=0)

    def one_expert(operands):
        members, expert_index = operands
        column_start = (expert_index * FF).astype(jnp.int32)
        gate_cols = lax.dynamic_slice_in_dim(w_gate, column_start, FF, 1)
        up_cols = lax.dynamic_slice_in_dim(w_up, column_start, FF, 1)
        down_rows = lax.dynamic_slice_in_dim(w_down, column_start, FF, 0)
        inputs = padded[members]
        gate_proj = jnp.dot(inputs, gate_cols, preferred_element_type=jnp.float32)
        up_proj = jnp.dot(inputs, up_cols, preferred_element_type=jnp.float32)
        activated = (jax.nn.silu(gate_proj) * up_proj).astype(jnp.bfloat16)
        summed = jnp.zeros((N_EP * ECAP, D), jnp.float32)
        for group_index in range(SPLIT):
            start_unit = group_index * HID_DEV
            slice_part = jnp.dot(activated[:, start_unit:start_unit + HID_DEV], down_rows[start_unit:start_unit + HID_DEV], preferred_element_type=jnp.float32).astype(jnp.bfloat16)
            summed = summed + lax.optimization_barrier(slice_part).astype(jnp.float32)
        return summed.astype(jnp.bfloat16)

    expert_out = lax.map(one_expert, (slot_rows, jnp.arange(EXPERTS, dtype=jnp.int32)))
    picked = expert_out[expert_ids, slot_of]
    moe_out = jnp.sum(gate_weights[:, :, None] * picked.astype(jnp.float32), axis=1).astype(jnp.bfloat16)

    parent_rows = (parents[:, 0] * REQUESTS + row_ids % REQUESTS).astype(jnp.int32)
    parent_len = lengths[parent_rows]
    parent_cache = latent_cache[parent_rows]
    token_place = jnp.arange(SUF, dtype=jnp.int32)[None, :, None]
    parent_bound = parent_len[:, None, None]
    appended = jnp.broadcast_to(new_latent[:, None, :], parent_cache.shape)
    new_cache = jnp.where(token_place < parent_bound, parent_cache, jnp.where(token_place == parent_bound, appended, jnp.zeros_like(parent_cache)))
    return moe_out, new_cache
```

```python
import jax
import jax.numpy as jnp
from jax import lax
from jax.sharding import PartitionSpec as P

D = 7168
TOP = 2
BEAMS = 8
SPLIT = 8
CAP = 2
LANES = 128


def passed_along(value, axis, by):
    peers = lax.axis_size(axis)
    return lax.ppermute(value, axis, [(i, (i + by) % peers) for i in range(peers)])


def swapped(value, mask):
    peers = lax.axis_size("ep")
    return lax.ppermute(value, "ep", [(i, i ^ mask) for i in range(peers)])


def dot32(a, b):
    return jnp.dot(a, b, preferred_element_type=jnp.float32)


def dense_local(
    hidden_rows,
    expert_ids,
    gate_weights,
    w_gate,
    w_up,
    w_down,
    latent_cache,
    new_latent,
    parents,
    lengths,
):
    device_count = lax.axis_size("ep")
    device_index = lax.axis_index("ep")
    experts = device_count // SPLIT
    rows = hidden_rows.shape[0]
    beam_stride = device_count // BEAMS
    own_beam = device_index // beam_stride
    own_expert = device_index // SPLIT
    bf16 = jnp.bfloat16

    tail = jnp.concatenate([parents, lengths[:, None]], axis=1).astype(bf16)
    tail = jnp.pad(tail, ((0, 0), (0, LANES - 2)))
    carried = jnp.concatenate([hidden_rows, tail], axis=1)
    own = jnp.concatenate(
        [carried] + [swapped(carried, SPLIT * k) for k in range(1, experts)], axis=0
    )
    quad = own.shape[0]
    half = quad // 2
    from_x = swapped(own, 2)
    from_y = swapped(own, 4)
    diag_a = swapped(from_x[:half, :D], 4)
    diag_b = swapped(from_y[half:, :D], 2)
    chip_rows = jnp.concatenate([own[:, :D], from_x[:, :D], from_y[:, :D], diag_a, diag_b], axis=0)
    other_rows = swapped(chip_rows, 1)

    meta = jnp.stack(
        [own[:, D : D + 2].reshape(experts, rows, 2), from_y[:, D : D + 2].reshape(experts, rows, 2)],
        axis=1,
    ).reshape(BEAMS, rows, 2)
    meta = meta.astype(jnp.int32)
    place = jnp.arange(BEAMS, dtype=jnp.int32)
    rank_range = jnp.arange(CAP, dtype=jnp.int32)
    wanted = meta[:, :, 0] == own_beam
    ranked = jnp.cumsum(wanted.astype(jnp.int32), axis=1) - 1
    selector = (
        (ranked[:, None, :] == rank_range[None, :, None]) & wanted[:, None, :]
    ).astype(bf16)
    selector = selector[place ^ own_beam]
    cache_flat = latent_cache.reshape(rows, -1)
    packets = dot32(selector.reshape(BEAMS * CAP, rows), cache_flat).astype(bf16)
    groups = [
        [b * beam_stride + r for b in range(BEAMS)] for r in range(beam_stride)
    ]
    arrived = lax.all_to_all(
        packets, "ep", split_axis=0, concat_axis=0, axis_index_groups=groups, tiled=True
    )

    def hidden_units(block):
        gate = dot32(block, w_gate)
        up = dot32(block, w_up)
        return (jax.nn.silu(gate) * up).astype(bf16)

    every = jnp.concatenate([chip_rows, other_rows], axis=0)
    act = hidden_units(every)
    chip = chip_rows.shape[0]
    leaving = dot32(act[chip:], w_down).astype(bf16)
    total = (dot32(act[:chip], w_down) + swapped(leaving, 1).astype(jnp.float32)).astype(bf16)
    mine, for_x, for_y, for_d = (total[i * quad : (i + 1) * quad] for i in range(4))
    got_a = swapped(for_d[:half], 2)
    got_b = swapped(for_d[half:], 4)
    f32 = jnp.float32
    for_y = jnp.concatenate(
        [(for_y[:half].astype(f32) + got_a.astype(f32)).astype(bf16), for_y[half:]], axis=0
    )
    for_x = jnp.concatenate(
        [for_x[:half], (for_x[half:].astype(f32) + got_b.astype(f32)).astype(bf16)], axis=0
    )
    back_x = swapped(for_x, 2)
    back_y = swapped(for_y, 4)
    summed = (mine.astype(f32) + back_x.astype(f32) + back_y.astype(f32)).astype(bf16)
    moe = None
    for k in range(experts):
        piece = summed[k * rows : (k + 1) * rows]
        if k:
            piece = swapped(piece, SPLIT * k)
        weight = jnp.sum(
            jnp.where(expert_ids == (own_expert ^ k), gate_weights, 0.0), axis=1, keepdims=True
        )
        term = weight * piece.astype(f32)
        moe = term if moe is None else moe + term
    moe_out = moe.astype(bf16)

    own_parents = parents[:, 0]
    from_beam = own_parents[None, :] == place[:, None]
    rank_in = jnp.cumsum(from_beam.astype(jnp.int32), axis=1) - 1
    picker = (
        from_beam[:, None, :] & (rank_in[:, None, :] == rank_range[None, :, None])
    ).astype(bf16)
    migrated = dot32(picker.reshape(BEAMS * CAP, rows).T, arrived).reshape(latent_cache.shape)
    by_place = (own_parents ^ own_beam)[None, :] == place[:, None]
    parent_len = jnp.sum(jnp.where(by_place, meta[:, :, 1], 0), axis=0)
    token_place = jnp.arange(latent_cache.shape[1], dtype=jnp.int32)[None, :, None]
    parent_bound = parent_len[:, None, None]
    appended = new_latent.astype(f32)[:, None, :]
    new_cache = jnp.where(
        token_place < parent_bound, migrated, jnp.where(token_place == parent_bound, appended, 0.0)
    ).astype(bf16)
    return (moe_out, new_cache)


def local(
    hidden_rows,
    expert_ids,
    gate_weights,
    w_gate,
    w_up,
    w_down,
    latent_cache,
    new_latent,
    parents,
    lengths,
):
    device_count = lax.axis_size("ep")
    device_index = lax.axis_index("ep")
    beam_stride = device_count // BEAMS
    own_beam = device_index // beam_stride
    request_block = device_index % beam_stride
    local_rows = hidden_rows.shape[0]
    experts = device_count // SPLIT
    capacity = max(2, min(local_rows, (2 * local_rows * TOP + experts - 1) // experts))
    if capacity == local_rows and experts & (experts - 1) == 0 and beam_stride * 2 == SPLIT:
        return dense_local(
            hidden_rows,
            expert_ids,
            gate_weights,
            w_gate,
            w_up,
            w_down,
            latent_cache,
            new_latent,
            parents,
            lengths,
        )
    expert_range = jnp.arange(experts, dtype=jnp.int32)
    chosen = expert_ids[:, :, None] == expert_range[None, None, :]
    hit_count = jnp.sum(chosen.astype(jnp.int32), axis=1)
    before = jnp.cumsum(hit_count, axis=0) - hit_count
    position = jnp.sum(jnp.where(chosen, before[:, None, :], 0), axis=2)
    slot_range = jnp.arange(capacity, dtype=jnp.int32)
    placer = (hit_count.T[:, None, :] == 1) & (before.T[:, None, :] == slot_range[None, :, None])
    outgoing = jnp.einsum(
        "ecr,rd->ecd", placer.astype(jnp.bfloat16), hidden_rows, preferred_element_type=jnp.float32
    ).astype(jnp.bfloat16)
    copies = jnp.broadcast_to(outgoing[:, None], (experts, SPLIT, capacity, D)).reshape(
        device_count, capacity, D
    )
    received = lax.all_to_all(copies, "ep", split_axis=0, concat_axis=0, tiled=True)
    item_count = received.shape[1]
    flat_rows = received.reshape(device_count * item_count, D)
    gate_proj = jnp.dot(flat_rows, w_gate, preferred_element_type=jnp.float32)
    up_proj = jnp.dot(flat_rows, w_up, preferred_element_type=jnp.float32)
    activated = (jax.nn.silu(gate_proj) * up_proj).astype(jnp.bfloat16)
    partial_value = jnp.dot(activated, w_down, preferred_element_type=jnp.float32).astype(
        jnp.bfloat16
    )
    partial_value = partial_value.reshape(device_count, item_count, D)
    result = lax.all_to_all(partial_value, "ep", split_axis=0, concat_axis=0, tiled=True)
    all_parents, all_lengths = (
        lax.all_gather(parents[:, 0], "ep", axis=0, tiled=True),
        lax.all_gather(lengths, "ep", axis=0, tiled=True),
    )
    parent_grid = lax.dynamic_index_in_dim(
        all_parents.reshape(BEAMS, beam_stride, local_rows), request_block, 1, keepdims=False
    )
    length_grid = lax.dynamic_index_in_dim(
        all_lengths.reshape(BEAMS, beam_stride, local_rows), request_block, 1, keepdims=False
    )
    cache_flat = latent_cache.reshape(local_rows, latent_cache.shape[1] * latent_cache.shape[2])
    packet_range = jnp.arange(CAP, dtype=jnp.int32)

    def selector(target_beam, source_beam):
        wanted = jnp.take(parent_grid, target_beam, axis=0) == source_beam
        ranked = jnp.cumsum(wanted.astype(jnp.int32)) - 1
        return ((ranked[None, :] == packet_range[:, None]) & wanted[None, :]).astype(jnp.bfloat16)

    def packet(target_beam):
        return jnp.dot(
            selector(target_beam, own_beam), cache_flat, preferred_element_type=jnp.float32
        ).astype(jnp.bfloat16)

    arrived = [packet(own_beam)]
    sources = [own_beam]
    for offset in range(1, BEAMS):
        arrived.append(
            passed_along(packet((own_beam + offset) % BEAMS), "ep", offset * beam_stride)
        )
        sources.append((own_beam - offset) % BEAMS)
    stacked = jnp.stack(arrived)
    pickers = jnp.stack([selector(own_beam, source_beam) for source_beam in sources])
    migrated = jnp.einsum(
        "acr,acf->rf", pickers, stacked, preferred_element_type=jnp.float32
    ).reshape(latent_cache.shape)
    own_parents = jnp.take(parent_grid, own_beam, axis=0)
    parent_len = jnp.sum(
        jnp.where(
            jnp.arange(BEAMS, dtype=jnp.int32)[:, None] == own_parents[None, :], length_grid, 0
        ),
        axis=0,
    )
    token_place = jnp.arange(latent_cache.shape[1], dtype=jnp.int32)[None, :, None]
    parent_bound = parent_len[:, None, None]
    appended = new_latent.astype(jnp.float32)[:, None, :]
    new_cache = jnp.where(
        token_place < parent_bound, migrated, jnp.where(token_place == parent_bound, appended, 0.0)
    ).astype(jnp.bfloat16)
    grouped = result.reshape(experts, SPLIT, capacity, D)
    expert_out = jnp.sum(grouped.astype(jnp.float32), axis=1).astype(jnp.bfloat16)
    flat_out = expert_out.reshape(experts * capacity, D)
    picked = flat_out[expert_ids * capacity + position]
    moe_out = jnp.sum(gate_weights[:, :, None] * picked.astype(jnp.float32), axis=1).astype(
        jnp.bfloat16
    )
    return (moe_out, new_cache)


def solution(mesh):
    placed = (
        P(("groups", "ep"), None),
        P(("groups", "ep"), None),
        P(("groups", "ep"), None),
        P(None, "ep"),
        P(None, "ep"),
        P("ep", None),
        P(("groups", "ep"), None, None),
        P(("groups", "ep"), None),
        P(("groups", "ep"), None),
        P(("groups", "ep")),
    )
    return jax.shard_map(
        local,
        mesh=mesh,
        in_specs=placed,
        out_specs=(P(("groups", "ep"), None), P(("groups", "ep"), None, None)),
        check_vma=False,
    )
```

```python
import jax
import jax.numpy as jnp
from jax import lax
from jax.experimental import pallas as pl
from jax.experimental.pallas import tpu as pltpu
from jax.sharding import PartitionSpec as P

D = 7168
TOP = 2
BEAMS = 8
SPLIT = 8
CAP = 2
CORE, X, Y = 1, 2, 4
LANES = 128
STEPS = 4
MIB = 1024 * 1024


def passed_along(value, axis, by):
    peers = lax.axis_size(axis)
    return lax.ppermute(value, axis, [(i, (i + by) % peers) for i in range(peers)])


def swapped(value, mask):
    peers = lax.axis_size("ep")
    return lax.ppermute(value, "ep", [(i, i ^ mask) for i in range(peers)])


def dot32(a, b):
    return jnp.dot(a, b, preferred_element_type=jnp.float32)


def in_vmem(value):
    return pltpu.with_memory_space_constraint(value, pltpu.VMEM)


def in_hbm(value):
    return pltpu.with_memory_space_constraint(value, pltpu.HBM)


def whole_call(body, ins, outs, limit=4, scratch=(), flops=0):
    whole = pl.BlockSpec(memory_space=pltpu.VMEM)
    far = pl.BlockSpec(memory_space=pltpu.HBM)
    arrays = [a[0] if isinstance(a, tuple) else a for a in ins]
    moved = sum(a.size * a.dtype.itemsize for a in arrays)
    return pl.pallas_call(
        body,
        in_specs=[far if isinstance(a, tuple) else whole for a in ins],
        out_specs=[whole] * len(outs),
        out_shape=[pltpu.VMEM(shape, dtype) for shape, dtype in outs],
        scratch_shapes=list(scratch),
        compiler_params=pltpu.CompilerParams(vmem_limit_bytes=limit * MIB),
        cost_estimate=pl.CostEstimate(flops=flops, bytes_accessed=moved, transcendentals=0),
    )(*[in_hbm(a[0]) if isinstance(a, tuple) else in_vmem(a) for a in ins])


def tailed_kernel(parents, lengths, rows, out):
    d = rows.shape[1]
    shape = (rows.shape[0], LANES)
    row = lax.broadcasted_iota(jnp.int32, shape, 0)
    lane = lax.broadcasted_iota(jnp.int32, shape, 1)
    tail = jnp.zeros(shape, jnp.int32)
    for i in range(shape[0]):
        tail = jnp.where((row == i) & (lane == 0), parents[i], tail)
        tail = jnp.where((row == i) & (lane == 1), lengths[i], tail)
    out[:, :d] = rows[...]
    out[:, d:] = tail.astype(jnp.float32).astype(out.dtype)


def tailed(rows, parents, lengths):
    count, d = rows.shape
    scalars = pl.BlockSpec(memory_space=pltpu.SMEM)
    whole = pl.BlockSpec(memory_space=pltpu.VMEM)
    return pl.pallas_call(
        tailed_kernel,
        in_specs=[scalars, scalars, whole],
        out_specs=whole,
        out_shape=pltpu.VMEM((count, d + LANES), rows.dtype),
        compiler_params=pltpu.CompilerParams(vmem_limit_bytes=2 * MIB),
        cost_estimate=pl.CostEstimate(flops=0, bytes_accessed=4 * count * d, transcendentals=0),
    )(parents, lengths, rows)


def stack_kernel(*refs):
    ins, out = refs[:-1], refs[-1]
    out[...] = jnp.concatenate([r[...].astype(jnp.float32) for r in ins], axis=0).astype(out.dtype)


def stacked(pieces):
    rows = sum(p.shape[0] for p in pieces)
    return whole_call(stack_kernel, pieces, [((rows, pieces[0].shape[1]), pieces[0].dtype)])[0]


def expert_math(rows, weights, near, far, gate_sum, up_sum, act):
    own, from_x, from_y, left, right = rows
    d = near.shape[1]
    chunk = d // STEPS
    half = left.shape[1]
    cuts = [slice(step * chunk, (step + 1) * chunk) for step in range(STEPS)]
    hid = gate_sum.shape[1] // len(weights)
    for core, (w_gate, w_up, _, ready) in enumerate(weights):
        units = slice(core * hid, (core + 1) * hid)
        for step, cut in enumerate(cuts):
            ready(step)
            corner = left[:, cut] if cut.stop <= half else right[:, cut.start - half : cut.stop - half]
            block = jnp.concatenate([own[:, cut], from_x[:, cut], from_y[:, cut], corner], axis=0)
            gate, up = dot32(block, w_gate[cut, :]), dot32(block, w_up[cut, :])
            if step:
                gate, up = gate_sum[:, units] + gate, up_sum[:, units] + up
            if step < STEPS - 1:
                gate_sum[:, units] = gate
                up_sum[:, units] = up
            else:
                act[:, units] = (gate / (1.0 + jnp.exp(-gate)) * up).astype(act.dtype)
    for _, _, _, ready in weights:
        ready(STEPS)
    rest = near.shape[0]
    for cut in cuts:
        part = sum(
            dot32(act[:, core * hid : (core + 1) * hid], w_down[:, cut])
            for core, (_, _, w_down, _) in enumerate(weights)
        ).astype(near.dtype)
        near[:, cut] = part[:rest]
        far[:, cut] = part[rest:]


def first_kernel(*refs):
    rows, sources, other = refs[:5], refs[5:8], refs[8:11]
    near, far = refs[11:13]
    held = refs[13:16]
    gate_sum, up_sum, act, sems = refs[16:]
    d = held[0].shape[0]
    chunk = d // STEPS
    steps = []
    for step in range(STEPS):
        cut = slice(step * chunk, (step + 1) * chunk)
        steps.append(
            [
                pltpu.make_async_copy(sources[i].at[cut, :], held[i].at[cut, :], sems.at[i, step])
                for i in range(2)
            ]
        )
    steps.append([pltpu.make_async_copy(sources[2], held[2], sems.at[2, 0])])
    for copies in steps:
        for copy in copies:
            copy.start()

    def ready(step):
        for copy in steps[step]:
            copy.wait()

    weights = [tuple(other) + (lambda step: None,), tuple(held) + (ready,)]
    expert_math(rows, weights, near, far, gate_sum, up_sum, act)


def second_kernel(*refs):
    rows, held, other = refs[:5], refs[5:8], refs[8:11]
    near, far, gate_sum, up_sum, act = refs[11:]
    weights = [tuple(w) + (lambda step: None,) for w in (other, held)]
    expert_math(rows, weights, near, far, gate_sum, up_sum, act)


def expert_outputs(rows, weights, other, first):
    quad = rows[0].shape[0]
    d, hid = weights[0].shape
    bf16, f32 = jnp.bfloat16, jnp.float32
    outs = [((3 * quad, d), bf16), ((quad, d), bf16)]
    scratch = [
        pltpu.VMEM((4 * quad, 2 * hid), f32),
        pltpu.VMEM((4 * quad, 2 * hid), f32),
        pltpu.VMEM((4 * quad, 2 * hid), bf16),
    ]
    flops = 2 * 4 * quad * d * 2 * hid * 3
    if first:
        outs = outs + [(w.shape, w.dtype) for w in weights]
        scratch.append(pltpu.SemaphoreType.DMA((3, STEPS)))
        ins = rows + [(w,) for w in weights] + other
        near, far, *held = whole_call(first_kernel, ins, outs, 8, scratch, flops)
        return near, far, held
    near, far = whole_call(second_kernel, rows + weights + other, outs, 8, scratch, flops)
    return near, far, weights


def join_kernel(near, got_a, got_b, mine, for_x, for_y):
    f32 = jnp.float32
    q = mine.shape[0]
    half = got_a.shape[1]
    mine[...] = near[:q, :]
    for_x[:, :half] = near[q : 2 * q, :half]
    for_x[:, half:] = (near[q : 2 * q, half:].astype(f32) + got_b[...].astype(f32)).astype(for_x.dtype)
    for_y[:, :half] = (near[2 * q :, :half].astype(f32) + got_a[...].astype(f32)).astype(for_y.dtype)
    for_y[:, half:] = near[2 * q :, half:]


def total_kernel(mine, back_x, back_y, *outs):
    f32 = jnp.float32
    total = mine[...].astype(f32) + back_x[...].astype(f32) + back_y[...].astype(f32)
    rows = outs[0].shape[0]
    for i, out in enumerate(outs):
        out[...] = total[i * rows : (i + 1) * rows].astype(out.dtype)


def read_facts(pieces, facts, scalars, sem):
    quad = pieces[0].shape[0]
    d = pieces[0].shape[1] - LANES
    for i, piece in enumerate(pieces):
        facts[i * quad : (i + 1) * quad, :] = piece[:, d:].astype(jnp.float32).astype(jnp.int32)
    copy = pltpu.make_async_copy(facts, scalars, sem)
    copy.start()
    copy.wait()


def fact_row(place, quad, rows):
    planes = quad // rows
    plane, side = place // 2, place % 2
    return ((plane // planes) * 2 + side) * quad + (plane % planes) * rows


def packing_kernel(who, own_a, y_a, own_b, y_b, cache, out, facts, scalars, sem):
    read_facts([own_a, y_a, own_b, y_b], facts, scalars, sem)
    rows = cache.shape[0]
    for place in range(BEAMS):
        at = fact_row(place, own_a.shape[0], rows)
        first = second = count = jnp.int32(0)
        for row in range(rows):
            hit = scalars[at + row, 0] == who[0]
            first = jnp.where(hit & (count == 0), row, first)
            second = jnp.where(hit & (count == 1), row, second)
            count = count + hit.astype(jnp.int32)
        for rank, pick in enumerate((first, second)):
            out[who[0] ^ place, rank] = cache[pick]


def unpacking_kernel(quad, who, facts, newest, arrived, out, scalars, sem):
    copy = pltpu.make_async_copy(facts, scalars, sem)
    copy.start()
    copy.wait()
    rows, tokens, width = out.shape
    planes = quad // rows
    for row in range(rows):
        parent = scalars[row, 0]
        rank = sum([(scalars[other, 0] == parent).astype(jnp.int32) for other in range(row)], jnp.int32(0))
        place = parent ^ who[0]
        plane, side = place // 2, place % 2
        at = ((plane // planes) * 2 + side) * quad + (plane % planes) * rows + row
        bound = scalars[at, 1]
        token = lax.broadcasted_iota(jnp.int32, (tokens, width), 0)
        old = arrived[parent, jnp.minimum(rank, CAP - 1)].astype(jnp.float32)
        value = jnp.where(token < bound, old, jnp.where(token == bound, newest[row], 0.0))
        out[row] = value.astype(out.dtype)


def packing_call(who, blocks, cache):
    whole = pl.BlockSpec(memory_space=pltpu.VMEM)
    table = (len(blocks) * blocks[0].shape[0], LANES)
    return pl.pallas_call(
        packing_kernel,
        in_specs=[pl.BlockSpec(memory_space=pltpu.SMEM)] + [whole] * (len(blocks) + 1),
        out_specs=[whole] * 2,
        out_shape=[
            jax.ShapeDtypeStruct((BEAMS, CAP) + cache.shape[1:], cache.dtype),
            pltpu.VMEM(table, jnp.int32),
        ],
        scratch_shapes=[pltpu.SMEM(table, jnp.int32), pltpu.SemaphoreType.DMA],
        compiler_params=pltpu.CompilerParams(vmem_limit_bytes=4 * MIB),
        cost_estimate=pl.CostEstimate(flops=0, bytes_accessed=4 * cache.size, transcendentals=0),
    )(who, *[in_vmem(b) for b in blocks], in_vmem(cache))


def unpacking_call(who, facts, quad, newest, arrived, shape):
    whole = pl.BlockSpec(memory_space=pltpu.VMEM)
    return pl.pallas_call(
        lambda *refs: unpacking_kernel(quad, *refs),
        in_specs=[pl.BlockSpec(memory_space=pltpu.SMEM)] + [whole] * 3,
        out_specs=whole,
        out_shape=shape,
        scratch_shapes=[pltpu.SMEM(facts.shape, jnp.int32), pltpu.SemaphoreType.DMA],
        compiler_params=pltpu.CompilerParams(vmem_limit_bytes=6 * MIB),
        cost_estimate=pl.CostEstimate(
            flops=0, bytes_accessed=4 * newest.size * shape.shape[1], transcendentals=0
        ),
    )(who, facts, newest, arrived)


def tied(*values):
    return lax.optimization_barrier(values)


def dense_local(
    hidden_rows,
    expert_ids,
    gate_weights,
    w_gate,
    w_up,
    w_down,
    latent_cache,
    new_latent,
    parents,
    lengths,
):
    device_count = lax.axis_size("ep")
    device_index = lax.axis_index("ep")
    experts = device_count // SPLIT
    rows, d = hidden_rows.shape
    half = d // 2
    beam_stride = device_count // BEAMS
    own_beam = device_index // beam_stride
    own_expert = device_index // SPLIT
    bf16 = jnp.bfloat16
    f32 = jnp.float32
    middle = experts // 2
    who = own_beam.reshape(1)

    other = [swapped(w_gate, CORE), swapped(w_up, CORE)]
    carried = tailed(hidden_rows, parents.reshape(rows), lengths)
    planes = [carried] + [swapped(carried, SPLIT * k) for k in range(1, experts)]
    own_a = stacked(planes[:middle])
    x_a, y_a = swapped(own_a, X), swapped(own_a, Y)
    x_a, y_a, planes[2], planes[3], w_down_out, *other[:2] = tied(x_a, y_a, planes[2], planes[3], w_down, *other[:2])
    other.append(swapped(w_down_out, CORE))
    rows_a = [own_a, x_a, y_a, swapped(x_a[:, :half], Y), swapped(y_a[:, half:d], X)]
    own_b = stacked(planes[middle:])
    x_b, y_b = swapped(own_b, X), swapped(own_b, Y)
    packets, facts = packing_call(who, [own_a, y_a, own_b, y_b], latent_cache)
    rows_b = [own_b, x_b, y_b, swapped(x_b[:, :half], Y), swapped(y_b[:, half:d], X)]
    groups = [[b * beam_stride + r for b in range(BEAMS)] for r in range(beam_stride)]
    arrived = lax.all_to_all(
        packets, "ep", split_axis=0, concat_axis=0, axis_index_groups=groups, tiled=True
    )

    near_a, far_a, held = expert_outputs(rows_a, [w_gate, w_up, w_down], other, True)
    near_b, far_b, _ = expert_outputs(rows_b, held, other, False)


    def joined(near, far):
        quad = far.shape[0]
        got_a, got_b = swapped(far[:, :half], X), swapped(far[:, half:], Y)
        return whole_call(join_kernel, [near, got_a, got_b], [((quad, d), bf16)] * 3)

    def totals(mine, for_x, for_y, count):
        return whole_call(
            total_kernel, [mine, swapped(for_x, X), swapped(for_y, Y)], [((rows, d), bf16)] * count
        )
    mine_b, to_x_b, to_y_b = joined(near_b, far_b)
    far_a, to_x_b, to_y_b = tied(far_a, to_x_b, to_y_b)
    sums_b = totals(mine_b, to_x_b, to_y_b, experts - middle)
    mine_a, to_x_a, to_y_a = joined(near_a, far_a)
    sums_a = totals(mine_a, to_x_a, to_y_a, middle)
    moe = None
    for k, piece in enumerate(list(sums_a) + list(sums_b)):
        if k:
            piece = swapped(piece, SPLIT * k)
        weight = jnp.sum(
            jnp.where(expert_ids == (own_expert ^ k), gate_weights, 0.0), axis=1, keepdims=True
        )
        term = weight * piece.astype(f32)
        moe = term if moe is None else moe + term
    moe_out = moe.astype(bf16)
    new_cache = unpacking_call(
        who,
        facts,
        own_a.shape[0],
        new_latent.astype(f32)[:, None, :],
        arrived,
        jax.ShapeDtypeStruct(latent_cache.shape, bf16),
    )
    return (moe_out, new_cache)


def local(
    hidden_rows,
    expert_ids,
    gate_weights,
    w_gate,
    w_up,
    w_down,
    latent_cache,
    new_latent,
    parents,
    lengths,
):
    device_count = lax.axis_size("ep")
    device_index = lax.axis_index("ep")
    beam_stride = device_count // BEAMS
    own_beam = device_index // beam_stride
    request_block = device_index % beam_stride
    local_rows = hidden_rows.shape[0]
    experts = device_count // SPLIT
    capacity = max(2, min(local_rows, (2 * local_rows * TOP + experts - 1) // experts))
    if capacity == local_rows and experts & (experts - 1) == 0 and beam_stride * 2 == SPLIT:
        return dense_local(
            hidden_rows,
            expert_ids,
            gate_weights,
            w_gate,
            w_up,
            w_down,
            latent_cache,
            new_latent,
            parents,
            lengths,
        )
    expert_range = jnp.arange(experts, dtype=jnp.int32)
    chosen = expert_ids[:, :, None] == expert_range[None, None, :]
    hit_count = jnp.sum(chosen.astype(jnp.int32), axis=1)
    before = jnp.cumsum(hit_count, axis=0) - hit_count
    position = jnp.sum(jnp.where(chosen, before[:, None, :], 0), axis=2)
    slot_range = jnp.arange(capacity, dtype=jnp.int32)
    placer = (hit_count.T[:, None, :] == 1) & (before.T[:, None, :] == slot_range[None, :, None])
    outgoing = jnp.einsum(
        "ecr,rd->ecd", placer.astype(jnp.bfloat16), hidden_rows, preferred_element_type=jnp.float32
    ).astype(jnp.bfloat16)
    copies = jnp.broadcast_to(outgoing[:, None], (experts, SPLIT, capacity, D)).reshape(
        device_count, capacity, D
    )
    received = lax.all_to_all(copies, "ep", split_axis=0, concat_axis=0, tiled=True)
    item_count = received.shape[1]
    flat_rows = received.reshape(device_count * item_count, D)
    gate_proj = jnp.dot(flat_rows, w_gate, preferred_element_type=jnp.float32)
    up_proj = jnp.dot(flat_rows, w_up, preferred_element_type=jnp.float32)
    activated = (jax.nn.silu(gate_proj) * up_proj).astype(jnp.bfloat16)
    partial_value = jnp.dot(activated, w_down, preferred_element_type=jnp.float32).astype(
        jnp.bfloat16
    )
    partial_value = partial_value.reshape(device_count, item_count, D)
    result = lax.all_to_all(partial_value, "ep", split_axis=0, concat_axis=0, tiled=True)
    all_parents, all_lengths = (
        lax.all_gather(parents[:, 0], "ep", axis=0, tiled=True),
        lax.all_gather(lengths, "ep", axis=0, tiled=True),
    )
    parent_grid = lax.dynamic_index_in_dim(
        all_parents.reshape(BEAMS, beam_stride, local_rows), request_block, 1, keepdims=False
    )
    length_grid = lax.dynamic_index_in_dim(
        all_lengths.reshape(BEAMS, beam_stride, local_rows), request_block, 1, keepdims=False
    )
    cache_flat = latent_cache.reshape(local_rows, latent_cache.shape[1] * latent_cache.shape[2])
    packet_range = jnp.arange(CAP, dtype=jnp.int32)

    def selector(target_beam, source_beam):
        wanted = jnp.take(parent_grid, target_beam, axis=0) == source_beam
        ranked = jnp.cumsum(wanted.astype(jnp.int32)) - 1
        return ((ranked[None, :] == packet_range[:, None]) & wanted[None, :]).astype(jnp.bfloat16)

    def packet(target_beam):
        return jnp.dot(
            selector(target_beam, own_beam), cache_flat, preferred_element_type=jnp.float32
        ).astype(jnp.bfloat16)

    arrived = [packet(own_beam)]
    sources = [own_beam]
    for offset in range(1, BEAMS):
        arrived.append(
            passed_along(packet((own_beam + offset) % BEAMS), "ep", offset * beam_stride)
        )
        sources.append((own_beam - offset) % BEAMS)
    stacked = jnp.stack(arrived)
    pickers = jnp.stack([selector(own_beam, source_beam) for source_beam in sources])
    migrated = jnp.einsum(
        "acr,acf->rf", pickers, stacked, preferred_element_type=jnp.float32
    ).reshape(latent_cache.shape)
    own_parents = jnp.take(parent_grid, own_beam, axis=0)
    parent_len = jnp.sum(
        jnp.where(
            jnp.arange(BEAMS, dtype=jnp.int32)[:, None] == own_parents[None, :], length_grid, 0
        ),
        axis=0,
    )
    token_place = jnp.arange(latent_cache.shape[1], dtype=jnp.int32)[None, :, None]
    parent_bound = parent_len[:, None, None]
    appended = new_latent.astype(jnp.float32)[:, None, :]
    new_cache = jnp.where(
        token_place < parent_bound, migrated, jnp.where(token_place == parent_bound, appended, 0.0)
    ).astype(jnp.bfloat16)
    grouped = result.reshape(experts, SPLIT, capacity, D)
    expert_out = jnp.sum(grouped.astype(jnp.float32), axis=1).astype(jnp.bfloat16)
    flat_out = expert_out.reshape(experts * capacity, D)
    picked = flat_out[expert_ids * capacity + position]
    moe_out = jnp.sum(gate_weights[:, :, None] * picked.astype(jnp.float32), axis=1).astype(
        jnp.bfloat16
    )
    return (moe_out, new_cache)


def solution(mesh):
    placed = (
        P(("groups", "ep"), None),
        P(("groups", "ep"), None),
        P(("groups", "ep"), None),
        P(None, "ep"),
        P(None, "ep"),
        P("ep", None),
        P(("groups", "ep"), None, None),
        P(("groups", "ep"), None),
        P(("groups", "ep"), None),
        P(("groups", "ep")),
    )
    return jax.shard_map(
        local,
        mesh=mesh,
        in_specs=placed,
        out_specs=(P(("groups", "ep"), None), P(("groups", "ep"), None, None)),
        check_vma=False,
    )
```

```python
import jax
import jax.numpy as jnp
from jax import lax
from jax.experimental import pallas as pl
from jax.experimental.pallas import tpu as pltpu
from jax.sharding import PartitionSpec as P

D = 7168
TOP = 2
BEAMS = 8
SPLIT = 8
CAP = 2
CORE, X, Y = 1, 2, 4
LANES = 128
STEPS = 4
MIB = 1024 * 1024


def passed_along(value, axis, by):
    peers = lax.axis_size(axis)
    return lax.ppermute(value, axis, [(i, (i + by) % peers) for i in range(peers)])


def swapped(value, mask):
    peers = lax.axis_size("ep")
    return lax.ppermute(value, "ep", [(i, i ^ mask) for i in range(peers)])


def dot32(a, b):
    return jnp.dot(a, b, preferred_element_type=jnp.float32)


def in_vmem(value):
    return pltpu.with_memory_space_constraint(value, pltpu.VMEM)


def in_hbm(value):
    return pltpu.with_memory_space_constraint(value, pltpu.HBM)


def whole_call(body, ins, outs, limit=4, scratch=(), flops=0):
    whole = pl.BlockSpec(memory_space=pltpu.VMEM)
    far = pl.BlockSpec(memory_space=pltpu.HBM)
    arrays = [a[0] if isinstance(a, tuple) else a for a in ins]
    moved = sum(a.size * a.dtype.itemsize for a in arrays)
    return pl.pallas_call(
        body,
        in_specs=[far if isinstance(a, tuple) else whole for a in ins],
        out_specs=[whole] * len(outs),
        out_shape=[pltpu.VMEM(shape, dtype) for shape, dtype in outs],
        scratch_shapes=list(scratch),
        compiler_params=pltpu.CompilerParams(vmem_limit_bytes=limit * MIB),
        cost_estimate=pl.CostEstimate(flops=flops, bytes_accessed=moved, transcendentals=0),
    )(*[in_hbm(a[0]) if isinstance(a, tuple) else in_vmem(a) for a in ins])


def tailed_kernel(parents, lengths, rows, out):
    d = rows.shape[1]
    shape = (rows.shape[0], LANES)
    row = lax.broadcasted_iota(jnp.int32, shape, 0)
    lane = lax.broadcasted_iota(jnp.int32, shape, 1)
    tail = jnp.zeros(shape, jnp.int32)
    for i in range(shape[0]):
        tail = jnp.where((row == i) & (lane == 0), parents[i], tail)
        tail = jnp.where((row == i) & (lane == 1), lengths[i], tail)
    out[:, :d] = rows[...]
    out[:, d:] = tail.astype(jnp.float32).astype(out.dtype)


def tailed(rows, parents, lengths):
    count, d = rows.shape
    scalars = pl.BlockSpec(memory_space=pltpu.SMEM)
    whole = pl.BlockSpec(memory_space=pltpu.VMEM)
    return pl.pallas_call(
        tailed_kernel,
        in_specs=[scalars, scalars, whole],
        out_specs=whole,
        out_shape=pltpu.VMEM((count, d + LANES), rows.dtype),
        compiler_params=pltpu.CompilerParams(vmem_limit_bytes=2 * MIB),
        cost_estimate=pl.CostEstimate(flops=0, bytes_accessed=4 * count * d, transcendentals=0),
    )(parents, lengths, rows)


def stack_kernel(*refs):
    ins, out = refs[:-1], refs[-1]
    out[...] = jnp.concatenate([r[...].astype(jnp.float32) for r in ins], axis=0).astype(out.dtype)


def stacked(pieces):
    rows = sum(p.shape[0] for p in pieces)
    return whole_call(stack_kernel, pieces, [((rows, pieces[0].shape[1]), pieces[0].dtype)])[0]


def expert_kernel(*refs):
    groups, sources, outs = (refs[:5], refs[5:10]), refs[10:16], refs[16:20]
    held, (gate_sum, up_sum, act, sems) = refs[20:26], refs[26:]
    d, hid = held[0].shape
    chunk = d // STEPS
    half = d // 2
    quad = groups[0][0].shape[0]
    cuts = [slice(step * chunk, (step + 1) * chunk) for step in range(STEPS)]
    copies = {}
    for core in range(2):
        for step, cut in enumerate(cuts):
            for i in range(2):
                at = 3 * core + i
                copies[at, step] = pltpu.make_async_copy(
                    sources[at].at[cut, :], held[at].at[cut, :], sems.at[at, step]
                )
    for core in range(2):
        at = 3 * core + 2
        copies[at, 0] = pltpu.make_async_copy(sources[at], held[at], sems.at[at, 0])
    for copy in copies.values():
        copy.start()
    for core in range(2):
        units = slice(core * hid, (core + 1) * hid)
        for step, cut in enumerate(cuts):
            blocks = []
            for own, from_x, from_y, left, right in groups:
                corner = left[:, cut] if cut.stop <= half else right[:, cut.start - half : cut.stop - half]
                blocks += [own[:, cut], from_x[:, cut], from_y[:, cut], corner]
            block = jnp.concatenate(blocks, axis=0)
            copies[3 * core, step].wait()
            gate = dot32(block, held[3 * core][cut, :])
            copies[3 * core + 1, step].wait()
            up = dot32(block, held[3 * core + 1][cut, :])
            if step:
                gate, up = gate_sum[...] + gate, up_sum[...] + up
            if step < STEPS - 1:
                gate_sum[...] = gate
                up_sum[...] = up
            else:
                act[:, units] = (gate / (1.0 + jnp.exp(-gate)) * up).astype(act.dtype)
    for core in range(2):
        copies[3 * core + 2, 0].wait()
    for cut in cuts:
        part = (dot32(act[:, :hid], held[2][:, cut]) + dot32(act[:, hid:], held[5][:, cut])).astype(outs[0].dtype)
        for i in range(2):
            start = 4 * quad * i
            outs[2 * i][:, cut] = part[start : start + 3 * quad]
            outs[2 * i + 1][:, cut] = part[start + 3 * quad : start + 4 * quad]


def expert_outputs(rows_a, rows_b, weights):
    quad = rows_a[0].shape[0]
    d, hid = weights[0].shape
    bf16, f32 = jnp.bfloat16, jnp.float32
    outs = [((3 * quad, d), bf16), ((quad, d), bf16)] * 2
    scratch = [pltpu.VMEM(w.shape, w.dtype) for w in weights] + [
        pltpu.VMEM((8 * quad, hid), f32),
        pltpu.VMEM((8 * quad, hid), f32),
        pltpu.VMEM((8 * quad, 2 * hid), bf16),
        pltpu.SemaphoreType.DMA((6, STEPS)),
    ]
    flops = 2 * 8 * quad * d * 2 * hid * 3
    return whole_call(expert_kernel, rows_a + rows_b + [(w,) for w in weights], outs, 32, scratch, flops)


def join_kernel(near, got_a, got_b, mine, for_x, for_y):
    f32 = jnp.float32
    q = mine.shape[0]
    half = got_a.shape[1]
    mine[...] = near[:q, :]
    for_x[:, :half] = near[q : 2 * q, :half]
    for_x[:, half:] = (near[q : 2 * q, half:].astype(f32) + got_b[...].astype(f32)).astype(for_x.dtype)
    for_y[:, :half] = (near[2 * q :, :half].astype(f32) + got_a[...].astype(f32)).astype(for_y.dtype)
    for_y[:, half:] = near[2 * q :, half:]


def total_kernel(mine, back_x, back_y, *outs):
    f32 = jnp.float32
    total = mine[...].astype(f32) + back_x[...].astype(f32) + back_y[...].astype(f32)
    rows = outs[0].shape[0]
    for i, out in enumerate(outs):
        out[...] = total[i * rows : (i + 1) * rows].astype(out.dtype)


def read_facts(pieces, facts, scalars, sem):
    quad = pieces[0].shape[0]
    d = pieces[0].shape[1] - LANES
    for i, piece in enumerate(pieces):
        facts[i * quad : (i + 1) * quad, :] = piece[:, d:].astype(jnp.float32).astype(jnp.int32)
    copy = pltpu.make_async_copy(facts, scalars, sem)
    copy.start()
    copy.wait()


def fact_row(place, quad, rows):
    planes = quad // rows
    plane, side = place // 2, place % 2
    return ((plane // planes) * 2 + side) * quad + (plane % planes) * rows


def own_beam():
    return lax.div(lax.axis_index("ep"), lax.axis_size("ep") // BEAMS)


def packing_kernel(own_a, y_a, own_b, y_b, cache, out, facts, scalars, sem):
    read_facts([own_a, y_a, own_b, y_b], facts, scalars, sem)
    rows = cache.shape[0]
    beam = own_beam()
    for place in range(BEAMS):
        at = fact_row(place, own_a.shape[0], rows)
        first = second = count = jnp.int32(0)
        for row in range(rows):
            hit = scalars[at + row, 0] == beam
            first = jnp.where(hit & (count == 0), row, first)
            second = jnp.where(hit & (count == 1), row, second)
            count = count + hit.astype(jnp.int32)
        for rank, pick in enumerate((first, second)):
            out[beam ^ place, rank] = cache[pick]


def unpacking_kernel(quad, facts, newest, arrived, out, scalars, sem):
    copy = pltpu.make_async_copy(facts, scalars, sem)
    copy.start()
    copy.wait()
    rows, tokens, width = out.shape
    planes = quad // rows
    beam = own_beam()
    for row in range(rows):
        parent = scalars[row, 0]
        rank = sum([(scalars[other, 0] == parent).astype(jnp.int32) for other in range(row)], jnp.int32(0))
        place = parent ^ beam
        plane, side = place // 2, place % 2
        at = ((plane // planes) * 2 + side) * quad + (plane % planes) * rows + row
        bound = scalars[at, 1]
        token = lax.broadcasted_iota(jnp.int32, (tokens, width), 0)
        old = arrived[parent, jnp.minimum(rank, CAP - 1)].astype(jnp.float32)
        value = jnp.where(token < bound, old, jnp.where(token == bound, newest[row], 0.0))
        out[row] = value.astype(out.dtype)


def packing_call(blocks, cache):
    whole = pl.BlockSpec(memory_space=pltpu.VMEM)
    table = (len(blocks) * blocks[0].shape[0], LANES)
    return pl.pallas_call(
        packing_kernel,
        in_specs=[whole] * (len(blocks) + 1),
        out_specs=[whole] * 2,
        out_shape=[
            jax.ShapeDtypeStruct((BEAMS, CAP) + cache.shape[1:], cache.dtype),
            pltpu.VMEM(table, jnp.int32),
        ],
        scratch_shapes=[pltpu.SMEM(table, jnp.int32), pltpu.SemaphoreType.DMA],
        compiler_params=pltpu.CompilerParams(vmem_limit_bytes=4 * MIB),
        cost_estimate=pl.CostEstimate(flops=0, bytes_accessed=4 * cache.size, transcendentals=0),
    )(*[in_vmem(b) for b in blocks], in_vmem(cache))


def unpacking_call(facts, quad, newest, arrived, shape):
    whole = pl.BlockSpec(memory_space=pltpu.VMEM)
    return pl.pallas_call(
        lambda *refs: unpacking_kernel(quad, *refs),
        in_specs=[whole] * 3,
        out_specs=whole,
        out_shape=shape,
        scratch_shapes=[pltpu.SMEM(facts.shape, jnp.int32), pltpu.SemaphoreType.DMA],
        compiler_params=pltpu.CompilerParams(vmem_limit_bytes=6 * MIB),
        cost_estimate=pl.CostEstimate(
            flops=0, bytes_accessed=4 * newest.size * shape.shape[1], transcendentals=0
        ),
    )(facts, newest, arrived)


def tied(*values):
    return lax.optimization_barrier(values)


def dense_local(
    hidden_rows,
    expert_ids,
    gate_weights,
    w_gate,
    w_up,
    w_down,
    latent_cache,
    new_latent,
    parents,
    lengths,
):
    device_count = lax.axis_size("ep")
    device_index = lax.axis_index("ep")
    experts = device_count // SPLIT
    rows, d = hidden_rows.shape
    half = d // 2
    beam_stride = device_count // BEAMS
    own_expert = device_index // SPLIT
    bf16 = jnp.bfloat16
    f32 = jnp.float32
    middle = experts // 2

    other = [swapped(w_gate, CORE), swapped(w_up, CORE)]
    carried = tailed(hidden_rows, parents.reshape(rows), lengths)
    planes = [carried] + [swapped(carried, SPLIT * k) for k in range(1, experts)]
    own_a = stacked(planes[:middle])
    x_a, y_a = swapped(own_a, X), swapped(own_a, Y)
    x_a, y_a, planes[2], planes[3], w_down_out, *other[:2] = tied(x_a, y_a, planes[2], planes[3], w_down, *other[:2])
    other.append(swapped(w_down_out, CORE))
    rows_a = [own_a, x_a, y_a, swapped(x_a[:, :half], Y), swapped(y_a[:, half:d], X)]
    own_b = stacked(planes[middle:])
    x_b, y_b = swapped(own_b, X), swapped(own_b, Y)
    packets, facts = packing_call([own_a, y_a, own_b, y_b], latent_cache)
    rows_b = [own_b, x_b, y_b, swapped(x_b[:, :half], Y), swapped(y_b[:, half:d], X)]
    groups = [[b * beam_stride + r for b in range(BEAMS)] for r in range(beam_stride)]
    arrived = lax.all_to_all(
        packets, "ep", split_axis=0, concat_axis=0, axis_index_groups=groups, tiled=True
    )

    near_a, far_a, near_b, far_b = expert_outputs(rows_a, rows_b, [w_gate, w_up, w_down] + other)


    def joined(near, far):
        quad = far.shape[0]
        got_a, got_b = swapped(far[:, :half], X), swapped(far[:, half:], Y)
        return whole_call(join_kernel, [near, got_a, got_b], [((quad, d), bf16)] * 3)

    def totals(mine, for_x, for_y, count):
        return whole_call(
            total_kernel, [mine, swapped(for_x, X), swapped(for_y, Y)], [((rows, d), bf16)] * count
        )
    mine_b, to_x_b, to_y_b = joined(near_b, far_b)
    far_a, to_x_b, to_y_b = tied(far_a, to_x_b, to_y_b)
    sums_b = totals(mine_b, to_x_b, to_y_b, experts - middle)
    mine_a, to_x_a, to_y_a = joined(near_a, far_a)
    sums_a = totals(mine_a, to_x_a, to_y_a, middle)
    moe = None
    for k, piece in enumerate(list(sums_a) + list(sums_b)):
        if k:
            piece = swapped(piece, SPLIT * k)
        weight = jnp.sum(
            jnp.where(expert_ids == (own_expert ^ k), gate_weights, 0.0), axis=1, keepdims=True
        )
        term = weight * piece.astype(f32)
        moe = term if moe is None else moe + term
    moe_out = moe.astype(bf16)
    new_cache = unpacking_call(
        facts,
        own_a.shape[0],
        new_latent.astype(f32)[:, None, :],
        arrived,
        jax.ShapeDtypeStruct(latent_cache.shape, bf16),
    )
    return (moe_out, new_cache)


def local(
    hidden_rows,
    expert_ids,
    gate_weights,
    w_gate,
    w_up,
    w_down,
    latent_cache,
    new_latent,
    parents,
    lengths,
):
    device_count = lax.axis_size("ep")
    device_index = lax.axis_index("ep")
    beam_stride = device_count // BEAMS
    own_beam = device_index // beam_stride
    request_block = device_index % beam_stride
    local_rows = hidden_rows.shape[0]
    experts = device_count // SPLIT
    capacity = max(2, min(local_rows, (2 * local_rows * TOP + experts - 1) // experts))
    if capacity == local_rows and experts & (experts - 1) == 0 and beam_stride * 2 == SPLIT:
        return dense_local(
            hidden_rows,
            expert_ids,
            gate_weights,
            w_gate,
            w_up,
            w_down,
            latent_cache,
            new_latent,
            parents,
            lengths,
        )
    expert_range = jnp.arange(experts, dtype=jnp.int32)
    chosen = expert_ids[:, :, None] == expert_range[None, None, :]
    hit_count = jnp.sum(chosen.astype(jnp.int32), axis=1)
    before = jnp.cumsum(hit_count, axis=0) - hit_count
    position = jnp.sum(jnp.where(chosen, before[:, None, :], 0), axis=2)
    slot_range = jnp.arange(capacity, dtype=jnp.int32)
    placer = (hit_count.T[:, None, :] == 1) & (before.T[:, None, :] == slot_range[None, :, None])
    outgoing = jnp.einsum(
        "ecr,rd->ecd", placer.astype(jnp.bfloat16), hidden_rows, preferred_element_type=jnp.float32
    ).astype(jnp.bfloat16)
    copies = jnp.broadcast_to(outgoing[:, None], (experts, SPLIT, capacity, D)).reshape(
        device_count, capacity, D
    )
    received = lax.all_to_all(copies, "ep", split_axis=0, concat_axis=0, tiled=True)
    item_count = received.shape[1]
    flat_rows = received.reshape(device_count * item_count, D)
    gate_proj = jnp.dot(flat_rows, w_gate, preferred_element_type=jnp.float32)
    up_proj = jnp.dot(flat_rows, w_up, preferred_element_type=jnp.float32)
    activated = (jax.nn.silu(gate_proj) * up_proj).astype(jnp.bfloat16)
    partial_value = jnp.dot(activated, w_down, preferred_element_type=jnp.float32).astype(
        jnp.bfloat16
    )
    partial_value = partial_value.reshape(device_count, item_count, D)
    result = lax.all_to_all(partial_value, "ep", split_axis=0, concat_axis=0, tiled=True)
    all_parents, all_lengths = (
        lax.all_gather(parents[:, 0], "ep", axis=0, tiled=True),
        lax.all_gather(lengths, "ep", axis=0, tiled=True),
    )
    parent_grid = lax.dynamic_index_in_dim(
        all_parents.reshape(BEAMS, beam_stride, local_rows), request_block, 1, keepdims=False
    )
    length_grid = lax.dynamic_index_in_dim(
        all_lengths.reshape(BEAMS, beam_stride, local_rows), request_block, 1, keepdims=False
    )
    cache_flat = latent_cache.reshape(local_rows, latent_cache.shape[1] * latent_cache.shape[2])
    packet_range = jnp.arange(CAP, dtype=jnp.int32)

    def selector(target_beam, source_beam):
        wanted = jnp.take(parent_grid, target_beam, axis=0) == source_beam
        ranked = jnp.cumsum(wanted.astype(jnp.int32)) - 1
        return ((ranked[None, :] == packet_range[:, None]) & wanted[None, :]).astype(jnp.bfloat16)

    def packet(target_beam):
        return jnp.dot(
            selector(target_beam, own_beam), cache_flat, preferred_element_type=jnp.float32
        ).astype(jnp.bfloat16)

    arrived = [packet(own_beam)]
    sources = [own_beam]
    for offset in range(1, BEAMS):
        arrived.append(
            passed_along(packet((own_beam + offset) % BEAMS), "ep", offset * beam_stride)
        )
        sources.append((own_beam - offset) % BEAMS)
    stacked = jnp.stack(arrived)
    pickers = jnp.stack([selector(own_beam, source_beam) for source_beam in sources])
    migrated = jnp.einsum(
        "acr,acf->rf", pickers, stacked, preferred_element_type=jnp.float32
    ).reshape(latent_cache.shape)
    own_parents = jnp.take(parent_grid, own_beam, axis=0)
    parent_len = jnp.sum(
        jnp.where(
            jnp.arange(BEAMS, dtype=jnp.int32)[:, None] == own_parents[None, :], length_grid, 0
        ),
        axis=0,
    )
    token_place = jnp.arange(latent_cache.shape[1], dtype=jnp.int32)[None, :, None]
    parent_bound = parent_len[:, None, None]
    appended = new_latent.astype(jnp.float32)[:, None, :]
    new_cache = jnp.where(
        token_place < parent_bound, migrated, jnp.where(token_place == parent_bound, appended, 0.0)
    ).astype(jnp.bfloat16)
    grouped = result.reshape(experts, SPLIT, capacity, D)
    expert_out = jnp.sum(grouped.astype(jnp.float32), axis=1).astype(jnp.bfloat16)
    flat_out = expert_out.reshape(experts * capacity, D)
    picked = flat_out[expert_ids * capacity + position]
    moe_out = jnp.sum(gate_weights[:, :, None] * picked.astype(jnp.float32), axis=1).astype(
        jnp.bfloat16
    )
    return (moe_out, new_cache)


def solution(mesh):
    placed = (
        P(("groups", "ep"), None),
        P(("groups", "ep"), None),
        P(("groups", "ep"), None),
        P(None, "ep"),
        P(None, "ep"),
        P("ep", None),
        P(("groups", "ep"), None, None),
        P(("groups", "ep"), None),
        P(("groups", "ep"), None),
        P(("groups", "ep")),
    )
    return jax.shard_map(
        local,
        mesh=mesh,
        in_specs=placed,
        out_specs=(P(("groups", "ep"), None), P(("groups", "ep"), None, None)),
        check_vma=False,
    )
```

```python
import jax
import jax.numpy as jnp
from jax import lax
from jax.experimental import pallas as pl
from jax.experimental.pallas import tpu as pltpu
from jax.sharding import PartitionSpec as P

D = 7168
TOP = 2
BEAMS = 8
SPLIT = 8
CAP = 2
CORE, X, Y = 1, 2, 4
LANES = 128
STEPS = 4
MIB = 1024 * 1024


def passed_along(value, axis, by):
    peers = lax.axis_size(axis)
    return lax.ppermute(value, axis, [(i, (i + by) % peers) for i in range(peers)])


def swapped(value, mask):
    peers = lax.axis_size("ep")
    return lax.ppermute(value, "ep", [(i, i ^ mask) for i in range(peers)])


def dot32(a, b):
    return jnp.dot(a, b, preferred_element_type=jnp.float32)


def in_vmem(value):
    return pltpu.with_memory_space_constraint(value, pltpu.VMEM)


def in_hbm(value):
    return pltpu.with_memory_space_constraint(value, pltpu.HBM)


def whole_call(body, ins, outs, limit=4, scratch=(), flops=0):
    whole = pl.BlockSpec(memory_space=pltpu.VMEM)
    far = pl.BlockSpec(memory_space=pltpu.HBM)
    arrays = [a[0] if isinstance(a, tuple) else a for a in ins]
    moved = sum(a.size * a.dtype.itemsize for a in arrays)
    return pl.pallas_call(
        body,
        in_specs=[far if isinstance(a, tuple) else whole for a in ins],
        out_specs=[whole] * len(outs),
        out_shape=[pltpu.VMEM(shape, dtype) for shape, dtype in outs],
        scratch_shapes=list(scratch),
        compiler_params=pltpu.CompilerParams(vmem_limit_bytes=limit * MIB),
        cost_estimate=pl.CostEstimate(flops=flops, bytes_accessed=moved, transcendentals=0),
    )(*[in_hbm(a[0]) if isinstance(a, tuple) else in_vmem(a) for a in ins])


def tailed_kernel(parents, lengths, rows, out, parent, length, sems):
    d = rows.shape[1]
    copies = [
        pltpu.make_async_copy(parents, parent, sems.at[0]),
        pltpu.make_async_copy(lengths, length, sems.at[1]),
        pltpu.make_async_copy(rows, out.at[:, pl.ds(0, d)], sems.at[2]),
    ]
    for copy in copies:
        copy.start()
    shape = (rows.shape[0], LANES)
    row = lax.broadcasted_iota(jnp.int32, shape, 0)
    lane = lax.broadcasted_iota(jnp.int32, shape, 1)
    tail = jnp.zeros(shape, jnp.int32)
    copies[0].wait()
    copies[1].wait()
    for i in range(shape[0]):
        tail = jnp.where((row == i) & (lane == 0), parent[i], tail)
        tail = jnp.where((row == i) & (lane == 1), length[i], tail)
    out[:, d:] = tail.astype(jnp.float32).astype(out.dtype)
    copies[2].wait()


def tailed(rows, parents, lengths):
    count, d = rows.shape
    return pl.pallas_call(
        tailed_kernel,
        in_specs=[pl.BlockSpec(memory_space=pltpu.HBM)] * 3,
        out_specs=pl.BlockSpec(memory_space=pltpu.VMEM),
        out_shape=pltpu.VMEM((count, d + LANES), rows.dtype),
        scratch_shapes=[
            pltpu.SMEM((count,), jnp.int32),
            pltpu.SMEM((count,), jnp.int32),
            pltpu.SemaphoreType.DMA((3,)),
        ],
        compiler_params=pltpu.CompilerParams(vmem_limit_bytes=2 * MIB),
        cost_estimate=pl.CostEstimate(flops=0, bytes_accessed=4 * count * d, transcendentals=0),
    )(in_hbm(parents), in_hbm(lengths), in_hbm(rows))


def stack_kernel(*refs):
    ins, out = refs[:-1], refs[-1]
    out[...] = jnp.concatenate([r[...].astype(jnp.float32) for r in ins], axis=0).astype(out.dtype)


def stacked(pieces):
    rows = sum(p.shape[0] for p in pieces)
    return whole_call(stack_kernel, pieces, [((rows, pieces[0].shape[1]), pieces[0].dtype)])[0]


def expert_kernel(*refs):
    groups, sources, outs = (refs[:5], refs[5:10]), refs[10:16], refs[16:20]
    held, (gate_sum, up_sum, act, sems) = refs[20:26], refs[26:]
    d, hid = held[0].shape
    chunk = d // STEPS
    half = d // 2
    quad = groups[0][0].shape[0]
    cuts = [slice(step * chunk, (step + 1) * chunk) for step in range(STEPS)]
    copies = {}
    for core in range(2):
        for step, cut in enumerate(cuts):
            for i in range(2):
                at = 3 * core + i
                copies[at, step] = pltpu.make_async_copy(
                    sources[at].at[cut, :], held[at].at[cut, :], sems.at[at, step]
                )
    for step, cut in enumerate(cuts):
        for at in (2, 5):
            copies[at, step] = pltpu.make_async_copy(
                sources[at].at[:, cut], held[at].at[:, cut], sems.at[at, step]
            )
    for copy in copies.values():
        copy.start()
    for core in range(2):
        units = slice(core * hid, (core + 1) * hid)
        for step, cut in enumerate(cuts):
            blocks = []
            for own, from_x, from_y, left, right in groups:
                corner = left[:, cut] if cut.stop <= half else right[:, cut.start - half : cut.stop - half]
                blocks += [own[:, cut], from_x[:, cut], from_y[:, cut], corner]
            block = jnp.concatenate(blocks, axis=0)
            copies[3 * core, step].wait()
            gate = dot32(block, held[3 * core][cut, :])
            copies[3 * core + 1, step].wait()
            up = dot32(block, held[3 * core + 1][cut, :])
            if step:
                gate, up = gate_sum[...] + gate, up_sum[...] + up
            if step < STEPS - 1:
                gate_sum[...] = gate
                up_sum[...] = up
            else:
                act[:, units] = (gate / (1.0 + jnp.exp(-gate)) * up).astype(act.dtype)
    for step, cut in enumerate(cuts):
        for at in (2, 5):
            copies[at, step].wait()
        part = (dot32(act[:, :hid], held[2][:, cut]) + dot32(act[:, hid:], held[5][:, cut])).astype(outs[0].dtype)
        for i in range(2):
            start = 4 * quad * i
            outs[2 * i][:, cut] = part[start : start + 3 * quad]
            outs[2 * i + 1][:, cut] = part[start + 3 * quad : start + 4 * quad]


def expert_outputs(rows_a, rows_b, weights):
    quad = rows_a[0].shape[0]
    d, hid = weights[0].shape
    bf16, f32 = jnp.bfloat16, jnp.float32
    outs = [((3 * quad, d), bf16), ((quad, d), bf16)] * 2
    scratch = [pltpu.VMEM(w.shape, w.dtype) for w in weights] + [
        pltpu.VMEM((8 * quad, hid), f32),
        pltpu.VMEM((8 * quad, hid), f32),
        pltpu.VMEM((8 * quad, 2 * hid), bf16),
        pltpu.SemaphoreType.DMA((6, STEPS)),
    ]
    flops = 2 * 8 * quad * d * 2 * hid * 3
    return whole_call(expert_kernel, rows_a + rows_b + [(w,) for w in weights], outs, 32, scratch, flops)


def join_kernel(near, got_a, got_b, mine, for_x, for_y):
    f32 = jnp.float32
    q = mine.shape[0]
    half = got_a.shape[1]
    mine[...] = near[:q, :]
    for_x[:, :half] = near[q : 2 * q, :half]
    for_x[:, half:] = (near[q : 2 * q, half:].astype(f32) + got_b[...].astype(f32)).astype(for_x.dtype)
    for_y[:, :half] = (near[2 * q :, :half].astype(f32) + got_a[...].astype(f32)).astype(for_y.dtype)
    for_y[:, half:] = near[2 * q :, half:]


def total_kernel(mine, back_x, back_y, *outs):
    f32 = jnp.float32
    total = mine[...].astype(f32) + back_x[...].astype(f32) + back_y[...].astype(f32)
    rows = outs[0].shape[0]
    for i, out in enumerate(outs):
        out[...] = total[i * rows : (i + 1) * rows].astype(out.dtype)


def read_facts(pieces, facts, scalars, sem):
    quad = pieces[0].shape[0]
    d = pieces[0].shape[1] - LANES
    for i, piece in enumerate(pieces):
        facts[i * quad : (i + 1) * quad, :] = piece[:, d:].astype(jnp.float32).astype(jnp.int32)
    copy = pltpu.make_async_copy(facts, scalars, sem)
    copy.start()
    copy.wait()


def fact_row(place, quad, rows):
    planes = quad // rows
    plane, side = place // 2, place % 2
    return ((plane // planes) * 2 + side) * quad + (plane % planes) * rows


def own_beam():
    return lax.div(lax.axis_index("ep"), lax.axis_size("ep") // BEAMS)


def packing_kernel(own_a, y_a, own_b, y_b, cache, out, facts, scalars, sem):
    read_facts([own_a, y_a, own_b, y_b], facts, scalars, sem)
    rows = cache.shape[0]
    beam = own_beam()
    for place in range(BEAMS):
        at = fact_row(place, own_a.shape[0], rows)
        first = second = count = jnp.int32(0)
        for row in range(rows):
            hit = scalars[at + row, 0] == beam
            first = jnp.where(hit & (count == 0), row, first)
            second = jnp.where(hit & (count == 1), row, second)
            count = count + hit.astype(jnp.int32)
        for rank, pick in enumerate((first, second)):
            out[beam ^ place, rank] = cache[pick]


def unpacking_kernel(quad, facts, newest, arrived, out, scalars, sem):
    copy = pltpu.make_async_copy(facts, scalars, sem)
    copy.start()
    copy.wait()
    rows, tokens, width = out.shape
    planes = quad // rows
    beam = own_beam()
    for row in range(rows):
        parent = scalars[row, 0]
        rank = sum([(scalars[other, 0] == parent).astype(jnp.int32) for other in range(row)], jnp.int32(0))
        place = parent ^ beam
        plane, side = place // 2, place % 2
        at = ((plane // planes) * 2 + side) * quad + (plane % planes) * rows + row
        bound = scalars[at, 1]
        token = lax.broadcasted_iota(jnp.int32, (tokens, width), 0)
        old = arrived[parent, jnp.minimum(rank, CAP - 1)].astype(jnp.float32)
        value = jnp.where(token < bound, old, jnp.where(token == bound, newest[row], 0.0))
        out[row] = value.astype(out.dtype)


def packing_call(blocks, cache):
    whole = pl.BlockSpec(memory_space=pltpu.VMEM)
    table = (len(blocks) * blocks[0].shape[0], LANES)
    return pl.pallas_call(
        packing_kernel,
        in_specs=[whole] * (len(blocks) + 1),
        out_specs=[whole] * 2,
        out_shape=[
            jax.ShapeDtypeStruct((BEAMS, CAP) + cache.shape[1:], cache.dtype),
            pltpu.VMEM(table, jnp.int32),
        ],
        scratch_shapes=[pltpu.SMEM(table, jnp.int32), pltpu.SemaphoreType.DMA],
        compiler_params=pltpu.CompilerParams(vmem_limit_bytes=4 * MIB),
        cost_estimate=pl.CostEstimate(flops=0, bytes_accessed=4 * cache.size, transcendentals=0),
    )(*[in_vmem(b) for b in blocks], in_vmem(cache))


def unpacking_call(facts, quad, newest, arrived, shape):
    whole = pl.BlockSpec(memory_space=pltpu.VMEM)
    return pl.pallas_call(
        lambda *refs: unpacking_kernel(quad, *refs),
        in_specs=[whole] * 3,
        out_specs=whole,
        out_shape=shape,
        scratch_shapes=[pltpu.SMEM(facts.shape, jnp.int32), pltpu.SemaphoreType.DMA],
        compiler_params=pltpu.CompilerParams(vmem_limit_bytes=6 * MIB),
        cost_estimate=pl.CostEstimate(
            flops=0, bytes_accessed=4 * newest.size * shape.shape[1], transcendentals=0
        ),
    )(facts, newest, arrived)


def tied(*values):
    return lax.optimization_barrier(values)


def dense_local(
    hidden_rows,
    expert_ids,
    gate_weights,
    w_gate,
    w_up,
    w_down,
    latent_cache,
    new_latent,
    parents,
    lengths,
):
    device_count = lax.axis_size("ep")
    device_index = lax.axis_index("ep")
    experts = device_count // SPLIT
    rows, d = hidden_rows.shape
    half = d // 2
    beam_stride = device_count // BEAMS
    own_expert = device_index // SPLIT
    bf16 = jnp.bfloat16
    f32 = jnp.float32
    middle = experts // 2

    other = [swapped(w_gate, CORE), swapped(w_up, CORE)]
    carried = tailed(hidden_rows, parents.reshape(rows), lengths)
    planes = [carried] + [swapped(carried, SPLIT * k) for k in range(1, experts)]
    own_a = stacked(planes[:middle])
    x_a, y_a = swapped(own_a, X), swapped(own_a, Y)
    x_a, y_a, planes[2], planes[3], w_down_out, *other[:2] = tied(x_a, y_a, planes[2], planes[3], w_down, *other[:2])
    other.append(swapped(w_down_out, CORE))
    rows_a = [own_a, x_a, y_a, swapped(x_a[:, :half], Y), swapped(y_a[:, half:d], X)]
    own_b = stacked(planes[middle:])
    x_b, y_b = swapped(own_b, X), swapped(own_b, Y)
    packets, facts = packing_call([own_a, y_a, own_b, y_b], latent_cache)
    rows_b = [own_b, x_b, y_b, swapped(x_b[:, :half], Y), swapped(y_b[:, half:d], X)]
    groups = [[b * beam_stride + r for b in range(BEAMS)] for r in range(beam_stride)]
    arrived = lax.all_to_all(
        packets, "ep", split_axis=0, concat_axis=0, axis_index_groups=groups, tiled=True
    )

    near_a, far_a, near_b, far_b = expert_outputs(rows_a, rows_b, [w_gate, w_up, w_down] + other)


    def joined(near, far):
        quad = far.shape[0]
        got_a, got_b = swapped(far[:, :half], X), swapped(far[:, half:], Y)
        return whole_call(join_kernel, [near, got_a, got_b], [((quad, d), bf16)] * 3)

    def totals(mine, for_x, for_y, count):
        return whole_call(
            total_kernel, [mine, swapped(for_x, X), swapped(for_y, Y)], [((rows, d), bf16)] * count
        )
    mine_b, to_x_b, to_y_b = joined(near_b, far_b)
    sums_b = totals(mine_b, to_x_b, to_y_b, experts - middle)
    mine_a, to_x_a, to_y_a = joined(near_a, far_a)
    sums_a = totals(mine_a, to_x_a, to_y_a, middle)
    moe = None
    for k, piece in enumerate(list(sums_a) + list(sums_b)):
        if k:
            piece = swapped(piece, SPLIT * k)
        weight = jnp.sum(
            jnp.where(expert_ids == (own_expert ^ k), gate_weights, 0.0), axis=1, keepdims=True
        )
        term = weight * piece.astype(f32)
        moe = term if moe is None else moe + term
    moe_out = moe.astype(bf16)
    new_cache = unpacking_call(
        facts,
        own_a.shape[0],
        new_latent.astype(f32)[:, None, :],
        arrived,
        jax.ShapeDtypeStruct(latent_cache.shape, bf16),
    )
    return (moe_out, new_cache)


def local(
    hidden_rows,
    expert_ids,
    gate_weights,
    w_gate,
    w_up,
    w_down,
    latent_cache,
    new_latent,
    parents,
    lengths,
):
    device_count = lax.axis_size("ep")
    device_index = lax.axis_index("ep")
    beam_stride = device_count // BEAMS
    own_beam = device_index // beam_stride
    request_block = device_index % beam_stride
    local_rows = hidden_rows.shape[0]
    experts = device_count // SPLIT
    capacity = max(2, min(local_rows, (2 * local_rows * TOP + experts - 1) // experts))
    if capacity == local_rows and experts & (experts - 1) == 0 and beam_stride * 2 == SPLIT:
        return dense_local(
            hidden_rows,
            expert_ids,
            gate_weights,
            w_gate,
            w_up,
            w_down,
            latent_cache,
            new_latent,
            parents,
            lengths,
        )
    expert_range = jnp.arange(experts, dtype=jnp.int32)
    chosen = expert_ids[:, :, None] == expert_range[None, None, :]
    hit_count = jnp.sum(chosen.astype(jnp.int32), axis=1)
    before = jnp.cumsum(hit_count, axis=0) - hit_count
    position = jnp.sum(jnp.where(chosen, before[:, None, :], 0), axis=2)
    slot_range = jnp.arange(capacity, dtype=jnp.int32)
    placer = (hit_count.T[:, None, :] == 1) & (before.T[:, None, :] == slot_range[None, :, None])
    outgoing = jnp.einsum(
        "ecr,rd->ecd", placer.astype(jnp.bfloat16), hidden_rows, preferred_element_type=jnp.float32
    ).astype(jnp.bfloat16)
    copies = jnp.broadcast_to(outgoing[:, None], (experts, SPLIT, capacity, D)).reshape(
        device_count, capacity, D
    )
    received = lax.all_to_all(copies, "ep", split_axis=0, concat_axis=0, tiled=True)
    item_count = received.shape[1]
    flat_rows = received.reshape(device_count * item_count, D)
    gate_proj = jnp.dot(flat_rows, w_gate, preferred_element_type=jnp.float32)
    up_proj = jnp.dot(flat_rows, w_up, preferred_element_type=jnp.float32)
    activated = (jax.nn.silu(gate_proj) * up_proj).astype(jnp.bfloat16)
    partial_value = jnp.dot(activated, w_down, preferred_element_type=jnp.float32).astype(
        jnp.bfloat16
    )
    partial_value = partial_value.reshape(device_count, item_count, D)
    result = lax.all_to_all(partial_value, "ep", split_axis=0, concat_axis=0, tiled=True)
    all_parents, all_lengths = (
        lax.all_gather(parents[:, 0], "ep", axis=0, tiled=True),
        lax.all_gather(lengths, "ep", axis=0, tiled=True),
    )
    parent_grid = lax.dynamic_index_in_dim(
        all_parents.reshape(BEAMS, beam_stride, local_rows), request_block, 1, keepdims=False
    )
    length_grid = lax.dynamic_index_in_dim(
        all_lengths.reshape(BEAMS, beam_stride, local_rows), request_block, 1, keepdims=False
    )
    cache_flat = latent_cache.reshape(local_rows, latent_cache.shape[1] * latent_cache.shape[2])
    packet_range = jnp.arange(CAP, dtype=jnp.int32)

    def selector(target_beam, source_beam):
        wanted = jnp.take(parent_grid, target_beam, axis=0) == source_beam
        ranked = jnp.cumsum(wanted.astype(jnp.int32)) - 1
        return ((ranked[None, :] == packet_range[:, None]) & wanted[None, :]).astype(jnp.bfloat16)

    def packet(target_beam):
        return jnp.dot(
            selector(target_beam, own_beam), cache_flat, preferred_element_type=jnp.float32
        ).astype(jnp.bfloat16)

    arrived = [packet(own_beam)]
    sources = [own_beam]
    for offset in range(1, BEAMS):
        arrived.append(
            passed_along(packet((own_beam + offset) % BEAMS), "ep", offset * beam_stride)
        )
        sources.append((own_beam - offset) % BEAMS)
    stacked = jnp.stack(arrived)
    pickers = jnp.stack([selector(own_beam, source_beam) for source_beam in sources])
    migrated = jnp.einsum(
        "acr,acf->rf", pickers, stacked, preferred_element_type=jnp.float32
    ).reshape(latent_cache.shape)
    own_parents = jnp.take(parent_grid, own_beam, axis=0)
    parent_len = jnp.sum(
        jnp.where(
            jnp.arange(BEAMS, dtype=jnp.int32)[:, None] == own_parents[None, :], length_grid, 0
        ),
        axis=0,
    )
    token_place = jnp.arange(latent_cache.shape[1], dtype=jnp.int32)[None, :, None]
    parent_bound = parent_len[:, None, None]
    appended = new_latent.astype(jnp.float32)[:, None, :]
    new_cache = jnp.where(
        token_place < parent_bound, migrated, jnp.where(token_place == parent_bound, appended, 0.0)
    ).astype(jnp.bfloat16)
    grouped = result.reshape(experts, SPLIT, capacity, D)
    expert_out = jnp.sum(grouped.astype(jnp.float32), axis=1).astype(jnp.bfloat16)
    flat_out = expert_out.reshape(experts * capacity, D)
    picked = flat_out[expert_ids * capacity + position]
    moe_out = jnp.sum(gate_weights[:, :, None] * picked.astype(jnp.float32), axis=1).astype(
        jnp.bfloat16
    )
    return (moe_out, new_cache)


def solution(mesh):
    placed = (
        P(("groups", "ep"), None),
        P(("groups", "ep"), None),
        P(("groups", "ep"), None),
        P(None, "ep"),
        P(None, "ep"),
        P("ep", None),
        P(("groups", "ep"), None, None),
        P(("groups", "ep"), None),
        P(("groups", "ep"), None),
        P(("groups", "ep")),
    )
    return jax.shard_map(
        local,
        mesh=mesh,
        in_specs=placed,
        out_specs=(P(("groups", "ep"), None), P(("groups", "ep"), None, None)),
        check_vma=False,
    )
```

```python
import jax
import jax.numpy as jnp
from jax import lax
from jax.experimental import pallas as pl
from jax.experimental.pallas import tpu as pltpu
from jax.sharding import PartitionSpec as P

D = 7168
TOP = 2
BEAMS = 8
SPLIT = 8
CAP = 2
CORE, X, Y = 1, 2, 4
LANES = 128
STEPS = 4
MIB = 1024 * 1024


def passed_along(value, axis, by):
    peers = lax.axis_size(axis)
    return lax.ppermute(value, axis, [(i, (i + by) % peers) for i in range(peers)])


def swapped(value, mask):
    peers = lax.axis_size("ep")
    return lax.ppermute(value, "ep", [(i, i ^ mask) for i in range(peers)])


def dot32(a, b):
    return jnp.dot(a, b, preferred_element_type=jnp.float32)


def in_vmem(value):
    return pltpu.with_memory_space_constraint(value, pltpu.VMEM)


def in_hbm(value):
    return pltpu.with_memory_space_constraint(value, pltpu.HBM)


def whole_call(body, ins, outs, limit=4, scratch=(), flops=0):
    whole = pl.BlockSpec(memory_space=pltpu.VMEM)
    far = pl.BlockSpec(memory_space=pltpu.HBM)
    arrays = [a[0] if isinstance(a, tuple) else a for a in ins]
    moved = sum(a.size * a.dtype.itemsize for a in arrays)
    return pl.pallas_call(
        body,
        in_specs=[far if isinstance(a, tuple) else whole for a in ins],
        out_specs=[whole] * len(outs),
        out_shape=[pltpu.VMEM(shape, dtype) for shape, dtype in outs],
        scratch_shapes=list(scratch),
        compiler_params=pltpu.CompilerParams(vmem_limit_bytes=limit * MIB),
        cost_estimate=pl.CostEstimate(flops=flops, bytes_accessed=moved, transcendentals=0),
    )(*[in_hbm(a[0]) if isinstance(a, tuple) else in_vmem(a) for a in ins])


def tailed_kernel(parents, lengths, rows, out, parent, length, sems):
    d = rows.shape[1]
    copies = [
        pltpu.make_async_copy(parents, parent, sems.at[0]),
        pltpu.make_async_copy(lengths, length, sems.at[1]),
        pltpu.make_async_copy(rows, out.at[:, pl.ds(0, d)], sems.at[2]),
    ]
    for copy in copies:
        copy.start()
    shape = (rows.shape[0], LANES)
    row = lax.broadcasted_iota(jnp.int32, shape, 0)
    lane = lax.broadcasted_iota(jnp.int32, shape, 1)
    tail = jnp.zeros(shape, jnp.int32)
    copies[0].wait()
    copies[1].wait()
    for i in range(shape[0]):
        tail = jnp.where((row == i) & (lane == 0), parent[i], tail)
        tail = jnp.where((row == i) & (lane == 1), length[i], tail)
    out[:, d:] = tail.astype(jnp.float32).astype(out.dtype)
    copies[2].wait()


def tailed(rows, parents, lengths):
    count, d = rows.shape
    return pl.pallas_call(
        tailed_kernel,
        in_specs=[pl.BlockSpec(memory_space=pltpu.HBM)] * 3,
        out_specs=pl.BlockSpec(memory_space=pltpu.VMEM),
        out_shape=pltpu.VMEM((count, d + LANES), rows.dtype),
        scratch_shapes=[
            pltpu.SMEM((count,), jnp.int32),
            pltpu.SMEM((count,), jnp.int32),
            pltpu.SemaphoreType.DMA((3,)),
        ],
        compiler_params=pltpu.CompilerParams(vmem_limit_bytes=2 * MIB),
        cost_estimate=pl.CostEstimate(flops=0, bytes_accessed=4 * count * d, transcendentals=0),
    )(in_hbm(parents), in_hbm(lengths), in_hbm(rows))


def stack_kernel(*refs):
    ins, out = refs[:-1], refs[-1]
    out[...] = jnp.concatenate([r[...].astype(jnp.float32) for r in ins], axis=0).astype(out.dtype)


def stacked(pieces):
    rows = sum(p.shape[0] for p in pieces)
    return whole_call(stack_kernel, pieces, [((rows, pieces[0].shape[1]), pieces[0].dtype)])[0]


def expert_kernel(*refs):
    groups, sources, outs = (refs[:5], refs[5:10]), refs[10:16], refs[16:20]
    held, (gate_sum, up_sum, act, sems) = refs[20:26], refs[26:]
    d, hid = held[0].shape
    chunk = d // STEPS
    half = d // 2
    quad = groups[0][0].shape[0]
    cuts = [slice(step * chunk, (step + 1) * chunk) for step in range(STEPS)]
    copies = {}
    for core in range(2):
        for step, cut in enumerate(cuts):
            for i in range(2):
                at = 3 * core + i
                copies[at, step] = pltpu.make_async_copy(
                    sources[at].at[cut, :], held[at].at[cut, :], sems.at[at, step]
                )
    for step, cut in enumerate(cuts):
        for at in (2, 5):
            copies[at, step] = pltpu.make_async_copy(
                sources[at].at[:, cut], held[at].at[:, cut], sems.at[at, step]
            )
    for copy in copies.values():
        copy.start()
    for core in range(2):
        units = slice(core * hid, (core + 1) * hid)
        for step, cut in enumerate(cuts):
            blocks = []
            for own, from_x, from_y, left, right in groups:
                corner = left[:, cut] if cut.stop <= half else right[:, cut.start - half : cut.stop - half]
                blocks += [own[:, cut], from_x[:, cut], from_y[:, cut], corner]
            block = jnp.concatenate(blocks, axis=0)
            copies[3 * core, step].wait()
            gate = dot32(block, held[3 * core][cut, :])
            copies[3 * core + 1, step].wait()
            up = dot32(block, held[3 * core + 1][cut, :])
            if step:
                gate, up = gate_sum[...] + gate, up_sum[...] + up
            if step < STEPS - 1:
                gate_sum[...] = gate
                up_sum[...] = up
            else:
                act[:, units] = (gate / (1.0 + jnp.exp(-gate)) * up).astype(act.dtype)
    for step, cut in enumerate(cuts):
        for at in (2, 5):
            copies[at, step].wait()
        part = (dot32(act[:, :hid], held[2][:, cut]) + dot32(act[:, hid:], held[5][:, cut])).astype(outs[0].dtype)
        for i in range(2):
            start = 4 * quad * i
            outs[2 * i][:, cut] = part[start : start + 3 * quad]
            outs[2 * i + 1][:, cut] = part[start + 3 * quad : start + 4 * quad]


def expert_outputs(rows_a, rows_b, weights):
    quad = rows_a[0].shape[0]
    d, hid = weights[0].shape
    bf16, f32 = jnp.bfloat16, jnp.float32
    outs = [((3 * quad, d), bf16), ((quad, d), bf16)] * 2
    scratch = [pltpu.VMEM(w.shape, w.dtype) for w in weights] + [
        pltpu.VMEM((8 * quad, hid), f32),
        pltpu.VMEM((8 * quad, hid), f32),
        pltpu.VMEM((8 * quad, 2 * hid), bf16),
        pltpu.SemaphoreType.DMA((6, STEPS)),
    ]
    flops = 2 * 8 * quad * d * 2 * hid * 3
    return whole_call(expert_kernel, rows_a + rows_b + [(w,) for w in weights], outs, 32, scratch, flops)


def join_kernel(near, got_a, got_b, mine, for_x, for_y):
    f32 = jnp.float32
    q = mine.shape[0]
    half = got_a.shape[1]
    mine[...] = near[:q, :]
    for_x[:, :half] = near[q : 2 * q, :half]
    for_x[:, half:] = (near[q : 2 * q, half:].astype(f32) + got_b[...].astype(f32)).astype(for_x.dtype)
    for_y[:, :half] = (near[2 * q :, :half].astype(f32) + got_a[...].astype(f32)).astype(for_y.dtype)
    for_y[:, half:] = near[2 * q :, half:]


def total_kernel(mine, back_x, back_y, *outs):
    f32 = jnp.float32
    total = mine[...].astype(f32) + back_x[...].astype(f32) + back_y[...].astype(f32)
    rows = outs[0].shape[0]
    for i, out in enumerate(outs):
        out[...] = total[i * rows : (i + 1) * rows].astype(out.dtype)


def read_facts(pieces, facts, scalars, sem):
    quad = pieces[0].shape[0]
    d = pieces[0].shape[1] - LANES
    for i, piece in enumerate(pieces):
        facts[i * quad : (i + 1) * quad, :] = piece[:, d:].astype(jnp.float32).astype(jnp.int32)
    copy = pltpu.make_async_copy(facts, scalars, sem)
    copy.start()
    copy.wait()


def fact_row(place, quad, rows):
    planes = quad // rows
    plane, side = place // 2, place % 2
    return ((plane // planes) * 2 + side) * quad + (plane % planes) * rows


def own_beam():
    return lax.div(lax.axis_index("ep"), lax.axis_size("ep") // BEAMS)


def packing_kernel(own_a, y_a, own_b, y_b, cache, out, facts, scalars, held, sem, cache_sem):
    fetch = pltpu.make_async_copy(cache, held, cache_sem)
    fetch.start()
    read_facts([own_a, y_a, own_b, y_b], facts, scalars, sem)
    rows = cache.shape[0]
    beam = own_beam()
    fetch.wait()
    for place in range(BEAMS):
        at = fact_row(place, own_a.shape[0], rows)
        first = second = count = jnp.int32(0)
        for row in range(rows):
            hit = scalars[at + row, 0] == beam
            first = jnp.where(hit & (count == 0), row, first)
            second = jnp.where(hit & (count == 1), row, second)
            count = count + hit.astype(jnp.int32)
        for rank, pick in enumerate((first, second)):
            out[beam ^ place, rank] = held[pick]


def unpacking_kernel(quad, facts, newest, arrived, out, scalars, sem):
    copy = pltpu.make_async_copy(facts, scalars, sem)
    copy.start()
    copy.wait()
    rows, tokens, width = out.shape
    planes = quad // rows
    beam = own_beam()
    for row in range(rows):
        parent = scalars[row, 0]
        rank = sum([(scalars[other, 0] == parent).astype(jnp.int32) for other in range(row)], jnp.int32(0))
        place = parent ^ beam
        plane, side = place // 2, place % 2
        at = ((plane // planes) * 2 + side) * quad + (plane % planes) * rows + row
        bound = scalars[at, 1]
        token = lax.broadcasted_iota(jnp.int32, (tokens, width), 0)
        old = arrived[parent, jnp.minimum(rank, CAP - 1)].astype(jnp.float32)
        value = jnp.where(token < bound, old, jnp.where(token == bound, newest[row], 0.0))
        out[row] = value.astype(out.dtype)


def packing_call(blocks, cache):
    whole = pl.BlockSpec(memory_space=pltpu.VMEM)
    table = (len(blocks) * blocks[0].shape[0], LANES)
    return pl.pallas_call(
        packing_kernel,
        in_specs=[whole] * len(blocks) + [pl.BlockSpec(memory_space=pltpu.HBM)],
        out_specs=[whole] * 2,
        out_shape=[
            jax.ShapeDtypeStruct((BEAMS, CAP) + cache.shape[1:], cache.dtype),
            pltpu.VMEM(table, jnp.int32),
        ],
        scratch_shapes=[
            pltpu.SMEM(table, jnp.int32),
            pltpu.VMEM(cache.shape, cache.dtype),
            pltpu.SemaphoreType.DMA,
            pltpu.SemaphoreType.DMA,
        ],
        compiler_params=pltpu.CompilerParams(vmem_limit_bytes=4 * MIB),
        cost_estimate=pl.CostEstimate(flops=0, bytes_accessed=4 * cache.size, transcendentals=0),
    )(*[in_vmem(b) for b in blocks], in_hbm(cache))


def unpacking_call(facts, quad, newest, arrived, shape):
    whole = pl.BlockSpec(memory_space=pltpu.VMEM)
    return pl.pallas_call(
        lambda *refs: unpacking_kernel(quad, *refs),
        in_specs=[whole] * 3,
        out_specs=whole,
        out_shape=shape,
        scratch_shapes=[pltpu.SMEM(facts.shape, jnp.int32), pltpu.SemaphoreType.DMA],
        compiler_params=pltpu.CompilerParams(vmem_limit_bytes=6 * MIB),
        cost_estimate=pl.CostEstimate(
            flops=0, bytes_accessed=4 * newest.size * shape.shape[1], transcendentals=0
        ),
    )(facts, newest, arrived)


def tied(*values):
    return lax.optimization_barrier(values)


def dense_local(
    hidden_rows,
    expert_ids,
    gate_weights,
    w_gate,
    w_up,
    w_down,
    latent_cache,
    new_latent,
    parents,
    lengths,
):
    device_count = lax.axis_size("ep")
    device_index = lax.axis_index("ep")
    experts = device_count // SPLIT
    rows, d = hidden_rows.shape
    half = d // 2
    beam_stride = device_count // BEAMS
    own_expert = device_index // SPLIT
    bf16 = jnp.bfloat16
    f32 = jnp.float32
    middle = experts // 2

    other = [swapped(w_gate, CORE), swapped(w_up, CORE)]
    carried = tailed(hidden_rows, parents.reshape(rows), lengths)
    planes = [carried] + [swapped(carried, SPLIT * k) for k in range(1, experts)]
    own_a = stacked(planes[:middle])
    x_a, y_a = swapped(own_a, X), swapped(own_a, Y)
    x_a, y_a, planes[2], planes[3], w_down_out, *other[:2] = tied(x_a, y_a, planes[2], planes[3], w_down, *other[:2])
    other.append(swapped(w_down_out, CORE))
    rows_a = [own_a, x_a, y_a, swapped(x_a[:, :half], Y), swapped(y_a[:, half:d], X)]
    own_b = stacked(planes[middle:])
    x_b, y_b = swapped(own_b, X), swapped(own_b, Y)
    packets, facts = packing_call([own_a, y_a, own_b, y_b], latent_cache)
    rows_b = [own_b, x_b, y_b, swapped(x_b[:, :half], Y), swapped(y_b[:, half:d], X)]
    groups = [[b * beam_stride + r for b in range(BEAMS)] for r in range(beam_stride)]
    arrived = lax.all_to_all(
        packets, "ep", split_axis=0, concat_axis=0, axis_index_groups=groups, tiled=True
    )

    near_a, far_a, near_b, far_b = expert_outputs(rows_a, rows_b, [w_gate, w_up, w_down] + other)


    def joined(near, far):
        quad = far.shape[0]
        got_a, got_b = swapped(far[:, :half], X), swapped(far[:, half:], Y)
        return whole_call(join_kernel, [near, got_a, got_b], [((quad, d), bf16)] * 3)

    def totals(mine, for_x, for_y, count):
        return whole_call(
            total_kernel, [mine, swapped(for_x, X), swapped(for_y, Y)], [((rows, d), bf16)] * count
        )
    mine_b, to_x_b, to_y_b = joined(near_b, far_b)
    sums_b = totals(mine_b, to_x_b, to_y_b, experts - middle)
    mine_a, to_x_a, to_y_a = joined(near_a, far_a)
    sums_a = totals(mine_a, to_x_a, to_y_a, middle)
    moe = None
    for k, piece in enumerate(list(sums_a) + list(sums_b)):
        if k:
            piece = swapped(piece, SPLIT * k)
        weight = jnp.sum(
            jnp.where(expert_ids == (own_expert ^ k), gate_weights, 0.0), axis=1, keepdims=True
        )
        term = weight * piece.astype(f32)
        moe = term if moe is None else moe + term
    moe_out = moe.astype(bf16)
    new_cache = unpacking_call(
        facts,
        own_a.shape[0],
        new_latent.astype(f32)[:, None, :],
        arrived,
        jax.ShapeDtypeStruct(latent_cache.shape, bf16),
    )
    return (moe_out, new_cache)


def local(
    hidden_rows,
    expert_ids,
    gate_weights,
    w_gate,
    w_up,
    w_down,
    latent_cache,
    new_latent,
    parents,
    lengths,
):
    device_count = lax.axis_size("ep")
    device_index = lax.axis_index("ep")
    beam_stride = device_count // BEAMS
    own_beam = device_index // beam_stride
    request_block = device_index % beam_stride
    local_rows = hidden_rows.shape[0]
    experts = device_count // SPLIT
    capacity = max(2, min(local_rows, (2 * local_rows * TOP + experts - 1) // experts))
    if capacity == local_rows and experts & (experts - 1) == 0 and beam_stride * 2 == SPLIT:
        return dense_local(
            hidden_rows,
            expert_ids,
            gate_weights,
            w_gate,
            w_up,
            w_down,
            latent_cache,
            new_latent,
            parents,
            lengths,
        )
    expert_range = jnp.arange(experts, dtype=jnp.int32)
    chosen = expert_ids[:, :, None] == expert_range[None, None, :]
    hit_count = jnp.sum(chosen.astype(jnp.int32), axis=1)
    before = jnp.cumsum(hit_count, axis=0) - hit_count
    position = jnp.sum(jnp.where(chosen, before[:, None, :], 0), axis=2)
    slot_range = jnp.arange(capacity, dtype=jnp.int32)
    placer = (hit_count.T[:, None, :] == 1) & (before.T[:, None, :] == slot_range[None, :, None])
    outgoing = jnp.einsum(
        "ecr,rd->ecd", placer.astype(jnp.bfloat16), hidden_rows, preferred_element_type=jnp.float32
    ).astype(jnp.bfloat16)
    copies = jnp.broadcast_to(outgoing[:, None], (experts, SPLIT, capacity, D)).reshape(
        device_count, capacity, D
    )
    received = lax.all_to_all(copies, "ep", split_axis=0, concat_axis=0, tiled=True)
    item_count = received.shape[1]
    flat_rows = received.reshape(device_count * item_count, D)
    gate_proj = jnp.dot(flat_rows, w_gate, preferred_element_type=jnp.float32)
    up_proj = jnp.dot(flat_rows, w_up, preferred_element_type=jnp.float32)
    activated = (jax.nn.silu(gate_proj) * up_proj).astype(jnp.bfloat16)
    partial_value = jnp.dot(activated, w_down, preferred_element_type=jnp.float32).astype(
        jnp.bfloat16
    )
    partial_value = partial_value.reshape(device_count, item_count, D)
    result = lax.all_to_all(partial_value, "ep", split_axis=0, concat_axis=0, tiled=True)
    all_parents, all_lengths = (
        lax.all_gather(parents[:, 0], "ep", axis=0, tiled=True),
        lax.all_gather(lengths, "ep", axis=0, tiled=True),
    )
    parent_grid = lax.dynamic_index_in_dim(
        all_parents.reshape(BEAMS, beam_stride, local_rows), request_block, 1, keepdims=False
    )
    length_grid = lax.dynamic_index_in_dim(
        all_lengths.reshape(BEAMS, beam_stride, local_rows), request_block, 1, keepdims=False
    )
    cache_flat = latent_cache.reshape(local_rows, latent_cache.shape[1] * latent_cache.shape[2])
    packet_range = jnp.arange(CAP, dtype=jnp.int32)

    def selector(target_beam, source_beam):
        wanted = jnp.take(parent_grid, target_beam, axis=0) == source_beam
        ranked = jnp.cumsum(wanted.astype(jnp.int32)) - 1
        return ((ranked[None, :] == packet_range[:, None]) & wanted[None, :]).astype(jnp.bfloat16)

    def packet(target_beam):
        return jnp.dot(
            selector(target_beam, own_beam), cache_flat, preferred_element_type=jnp.float32
        ).astype(jnp.bfloat16)

    arrived = [packet(own_beam)]
    sources = [own_beam]
    for offset in range(1, BEAMS):
        arrived.append(
            passed_along(packet((own_beam + offset) % BEAMS), "ep", offset * beam_stride)
        )
        sources.append((own_beam - offset) % BEAMS)
    stacked = jnp.stack(arrived)
    pickers = jnp.stack([selector(own_beam, source_beam) for source_beam in sources])
    migrated = jnp.einsum(
        "acr,acf->rf", pickers, stacked, preferred_element_type=jnp.float32
    ).reshape(latent_cache.shape)
    own_parents = jnp.take(parent_grid, own_beam, axis=0)
    parent_len = jnp.sum(
        jnp.where(
            jnp.arange(BEAMS, dtype=jnp.int32)[:, None] == own_parents[None, :], length_grid, 0
        ),
        axis=0,
    )
    token_place = jnp.arange(latent_cache.shape[1], dtype=jnp.int32)[None, :, None]
    parent_bound = parent_len[:, None, None]
    appended = new_latent.astype(jnp.float32)[:, None, :]
    new_cache = jnp.where(
        token_place < parent_bound, migrated, jnp.where(token_place == parent_bound, appended, 0.0)
    ).astype(jnp.bfloat16)
    grouped = result.reshape(experts, SPLIT, capacity, D)
    expert_out = jnp.sum(grouped.astype(jnp.float32), axis=1).astype(jnp.bfloat16)
    flat_out = expert_out.reshape(experts * capacity, D)
    picked = flat_out[expert_ids * capacity + position]
    moe_out = jnp.sum(gate_weights[:, :, None] * picked.astype(jnp.float32), axis=1).astype(
        jnp.bfloat16
    )
    return (moe_out, new_cache)


def solution(mesh):
    placed = (
        P(("groups", "ep"), None),
        P(("groups", "ep"), None),
        P(("groups", "ep"), None),
        P(None, "ep"),
        P(None, "ep"),
        P("ep", None),
        P(("groups", "ep"), None, None),
        P(("groups", "ep"), None),
        P(("groups", "ep"), None),
        P(("groups", "ep")),
    )
    return jax.shard_map(
        local,
        mesh=mesh,
        in_specs=placed,
        out_specs=(P(("groups", "ep"), None), P(("groups", "ep"), None, None)),
        check_vma=False,
    )
```

```python
import jax
import jax.numpy as jnp
from jax import lax
from jax.experimental import pallas as pl
from jax.experimental.pallas import tpu as pltpu
from jax.sharding import PartitionSpec as P

D = 7168
TOP = 2
BEAMS = 8
SPLIT = 8
CAP = 2
CORE, X, Y = 1, 2, 4
LANES = 128
STEPS = 4
MIB = 1024 * 1024


def passed_along(value, axis, by):
    peers = lax.axis_size(axis)
    return lax.ppermute(value, axis, [(i, (i + by) % peers) for i in range(peers)])


def swapped(value, mask):
    peers = lax.axis_size("ep")
    return lax.ppermute(value, "ep", [(i, i ^ mask) for i in range(peers)])


def dot32(a, b):
    return jnp.dot(a, b, preferred_element_type=jnp.float32)


def in_vmem(value):
    return pltpu.with_memory_space_constraint(value, pltpu.VMEM)


def in_hbm(value):
    return pltpu.with_memory_space_constraint(value, pltpu.HBM)


def whole_call(body, ins, outs, limit=4, scratch=(), flops=0):
    whole = pl.BlockSpec(memory_space=pltpu.VMEM)
    far = pl.BlockSpec(memory_space=pltpu.HBM)
    arrays = [a[0] if isinstance(a, tuple) else a for a in ins]
    moved = sum(a.size * a.dtype.itemsize for a in arrays)
    return pl.pallas_call(
        body,
        in_specs=[far if isinstance(a, tuple) else whole for a in ins],
        out_specs=[whole] * len(outs),
        out_shape=[pltpu.VMEM(shape, dtype) for shape, dtype in outs],
        scratch_shapes=list(scratch),
        compiler_params=pltpu.CompilerParams(vmem_limit_bytes=limit * MIB),
        cost_estimate=pl.CostEstimate(flops=flops, bytes_accessed=moved, transcendentals=0),
    )(*[in_hbm(a[0]) if isinstance(a, tuple) else in_vmem(a) for a in ins])


def tailed_kernel(parents, lengths, rows, out, parent, length, sems):
    d = rows.shape[1]
    copies = [
        pltpu.make_async_copy(parents, parent, sems.at[0]),
        pltpu.make_async_copy(lengths, length, sems.at[1]),
        pltpu.make_async_copy(rows, out.at[:, pl.ds(0, d)], sems.at[2]),
    ]
    for copy in copies:
        copy.start()
    shape = (rows.shape[0], LANES)
    row = lax.broadcasted_iota(jnp.int32, shape, 0)
    lane = lax.broadcasted_iota(jnp.int32, shape, 1)
    tail = jnp.zeros(shape, jnp.int32)
    copies[0].wait()
    copies[1].wait()
    for i in range(shape[0]):
        tail = jnp.where((row == i) & (lane == 0), parent[i], tail)
        tail = jnp.where((row == i) & (lane == 1), length[i], tail)
    out[:, d:] = tail.astype(jnp.float32).astype(out.dtype)
    copies[2].wait()


def tailed(rows, parents, lengths):
    count, d = rows.shape
    return pl.pallas_call(
        tailed_kernel,
        in_specs=[pl.BlockSpec(memory_space=pltpu.HBM)] * 3,
        out_specs=pl.BlockSpec(memory_space=pltpu.VMEM),
        out_shape=pltpu.VMEM((count, d + LANES), rows.dtype),
        scratch_shapes=[
            pltpu.SMEM((count,), jnp.int32),
            pltpu.SMEM((count,), jnp.int32),
            pltpu.SemaphoreType.DMA((3,)),
        ],
        compiler_params=pltpu.CompilerParams(vmem_limit_bytes=2 * MIB),
        cost_estimate=pl.CostEstimate(flops=0, bytes_accessed=4 * count * d, transcendentals=0),
    )(in_hbm(parents), in_hbm(lengths), in_hbm(rows))


def stack_kernel(*refs):
    ins, out = refs[:-1], refs[-1]
    out[...] = jnp.concatenate([r[...].astype(jnp.float32) for r in ins], axis=0).astype(out.dtype)


def stacked(pieces):
    rows = sum(p.shape[0] for p in pieces)
    return whole_call(stack_kernel, pieces, [((rows, pieces[0].shape[1]), pieces[0].dtype)])[0]


def expert_kernel(*refs):
    groups, sources, outs = (refs[:5], refs[5:10]), refs[10:16], refs[16:20]
    held, (gate_sum, up_sum, act, sems) = refs[20:26], refs[26:]
    d, hid = held[0].shape
    chunk = d // STEPS
    half = d // 2
    quad = groups[0][0].shape[0]
    cuts = [slice(step * chunk, (step + 1) * chunk) for step in range(STEPS)]
    copies = {}
    for core in range(2):
        for step, cut in enumerate(cuts):
            for i in range(2):
                at = 3 * core + i
                copies[at, step] = pltpu.make_async_copy(
                    sources[at].at[cut, :], held[at].at[cut, :], sems.at[at, step]
                )
    for step, cut in enumerate(cuts):
        for at in (2, 5):
            copies[at, step] = pltpu.make_async_copy(
                sources[at].at[:, cut], held[at].at[:, cut], sems.at[at, step]
            )
    for copy in copies.values():
        copy.start()
    for core in range(2):
        units = slice(core * hid, (core + 1) * hid)
        for step, cut in enumerate(cuts):
            blocks = []
            for own, from_x, from_y, left, right in groups:
                corner = left[:, cut] if cut.stop <= half else right[:, cut.start - half : cut.stop - half]
                blocks += [own[:, cut], from_x[:, cut], from_y[:, cut], corner]
            block = jnp.concatenate(blocks, axis=0)
            copies[3 * core, step].wait()
            gate = dot32(block, held[3 * core][cut, :])
            copies[3 * core + 1, step].wait()
            up = dot32(block, held[3 * core + 1][cut, :])
            if step:
                gate, up = gate_sum[...] + gate, up_sum[...] + up
            if step < STEPS - 1:
                gate_sum[...] = gate
                up_sum[...] = up
            else:
                act[:, units] = (gate / (1.0 + jnp.exp(-gate)) * up).astype(act.dtype)
    for step, cut in enumerate(cuts):
        for at in (2, 5):
            copies[at, step].wait()
        part = (dot32(act[:, :hid], held[2][:, cut]) + dot32(act[:, hid:], held[5][:, cut])).astype(outs[0].dtype)
        for i in range(2):
            start = 4 * quad * i
            outs[2 * i][:, cut] = part[start : start + 3 * quad]
            outs[2 * i + 1][:, cut] = part[start + 3 * quad : start + 4 * quad]


def expert_outputs(rows_a, rows_b, weights):
    quad = rows_a[0].shape[0]
    d, hid = weights[0].shape
    bf16, f32 = jnp.bfloat16, jnp.float32
    outs = [((3 * quad, d), bf16), ((quad, d), bf16)] * 2
    scratch = [pltpu.VMEM(w.shape, w.dtype) for w in weights] + [
        pltpu.VMEM((8 * quad, hid), f32),
        pltpu.VMEM((8 * quad, hid), f32),
        pltpu.VMEM((8 * quad, 2 * hid), bf16),
        pltpu.SemaphoreType.DMA((6, STEPS)),
    ]
    flops = 2 * 8 * quad * d * 2 * hid * 3
    return whole_call(expert_kernel, rows_a + rows_b + [(w,) for w in weights], outs, 32, scratch, flops)


def join_kernel(near, got_a, got_b, mine, for_x, for_y):
    f32 = jnp.float32
    q = mine.shape[0]
    half = got_a.shape[1]
    mine[...] = near[:q, :]
    for_x[:, :half] = near[q : 2 * q, :half]
    for_x[:, half:] = (near[q : 2 * q, half:].astype(f32) + got_b[...].astype(f32)).astype(for_x.dtype)
    for_y[:, :half] = (near[2 * q :, :half].astype(f32) + got_a[...].astype(f32)).astype(for_y.dtype)
    for_y[:, half:] = near[2 * q :, half:]


def total_kernel(mine, back_x, back_y, *outs):
    f32 = jnp.float32
    total = mine[...].astype(f32) + back_x[...].astype(f32) + back_y[...].astype(f32)
    rows = outs[0].shape[0]
    for i, out in enumerate(outs):
        out[...] = total[i * rows : (i + 1) * rows].astype(out.dtype)


def read_facts(pieces, facts, scalars, sem):
    quad = pieces[0].shape[0]
    d = pieces[0].shape[1] - LANES
    for i, piece in enumerate(pieces):
        facts[i * quad : (i + 1) * quad, :] = piece[:, d:].astype(jnp.float32).astype(jnp.int32)
    copy = pltpu.make_async_copy(facts, scalars, sem)
    copy.start()
    copy.wait()


def fact_row(place, quad, rows):
    planes = quad // rows
    plane, side = place // 2, place % 2
    return ((plane // planes) * 2 + side) * quad + (plane % planes) * rows


def own_beam():
    return lax.div(lax.axis_index("ep"), lax.axis_size("ep") // BEAMS)


def packing_kernel(own_a, y_a, own_b, y_b, cache, out, facts, scalars, held, sem, cache_sem):
    fetch = pltpu.make_async_copy(cache, held, cache_sem)
    fetch.start()
    read_facts([own_a, y_a, own_b, y_b], facts, scalars, sem)
    rows = cache.shape[0]
    beam = own_beam()
    fetch.wait()
    for place in range(BEAMS):
        at = fact_row(place, own_a.shape[0], rows)
        first = second = count = jnp.int32(0)
        for row in range(rows):
            hit = scalars[at + row, 0] == beam
            first = jnp.where(hit & (count == 0), row, first)
            second = jnp.where(hit & (count == 1), row, second)
            count = count + hit.astype(jnp.int32)
        pair = [held[pick].astype(jnp.float32) for pick in (first, second)]
        out[beam ^ place] = jnp.concatenate(pair, axis=1).astype(out.dtype)


def unpacking_kernel(quad, facts, newest, arrived, out, scalars, sem):
    copy = pltpu.make_async_copy(facts, scalars, sem)
    copy.start()
    copy.wait()
    rows, tokens, width = out.shape
    planes = quad // rows
    beam = own_beam()
    for row in range(rows):
        parent = scalars[row, 0]
        rank = sum([(scalars[other, 0] == parent).astype(jnp.int32) for other in range(row)], jnp.int32(0))
        place = parent ^ beam
        plane, side = place // 2, place % 2
        at = ((plane // planes) * 2 + side) * quad + (plane % planes) * rows + row
        bound = scalars[at, 1]
        token = lax.broadcasted_iota(jnp.int32, (tokens, width), 0)
        pair = arrived[parent].astype(jnp.float32)
        old = jnp.where(rank == 0, pair[:, :width], pair[:, width:])
        value = jnp.where(token < bound, old, jnp.where(token == bound, newest[row], 0.0))
        out[row] = value.astype(out.dtype)


def packing_call(blocks, cache):
    whole = pl.BlockSpec(memory_space=pltpu.VMEM)
    table = (len(blocks) * blocks[0].shape[0], LANES)
    return pl.pallas_call(
        packing_kernel,
        in_specs=[whole] * len(blocks) + [pl.BlockSpec(memory_space=pltpu.HBM)],
        out_specs=[whole] * 2,
        out_shape=[
            jax.ShapeDtypeStruct((BEAMS, cache.shape[1], CAP * cache.shape[2]), cache.dtype),
            pltpu.VMEM(table, jnp.int32),
        ],
        scratch_shapes=[
            pltpu.SMEM(table, jnp.int32),
            pltpu.VMEM(cache.shape, cache.dtype),
            pltpu.SemaphoreType.DMA,
            pltpu.SemaphoreType.DMA,
        ],
        compiler_params=pltpu.CompilerParams(vmem_limit_bytes=4 * MIB),
        cost_estimate=pl.CostEstimate(flops=0, bytes_accessed=4 * cache.size, transcendentals=0),
    )(*[in_vmem(b) for b in blocks], in_hbm(cache))


def unpacking_call(facts, quad, newest, arrived, shape):
    whole = pl.BlockSpec(memory_space=pltpu.VMEM)
    return pl.pallas_call(
        lambda *refs: unpacking_kernel(quad, *refs),
        in_specs=[whole] * 3,
        out_specs=whole,
        out_shape=shape,
        scratch_shapes=[pltpu.SMEM(facts.shape, jnp.int32), pltpu.SemaphoreType.DMA],
        compiler_params=pltpu.CompilerParams(vmem_limit_bytes=6 * MIB),
        cost_estimate=pl.CostEstimate(
            flops=0, bytes_accessed=4 * newest.size * shape.shape[1], transcendentals=0
        ),
    )(facts, newest, arrived)


def tied(*values):
    return lax.optimization_barrier(values)


def dense_local(
    hidden_rows,
    expert_ids,
    gate_weights,
    w_gate,
    w_up,
    w_down,
    latent_cache,
    new_latent,
    parents,
    lengths,
):
    device_count = lax.axis_size("ep")
    device_index = lax.axis_index("ep")
    experts = device_count // SPLIT
    rows, d = hidden_rows.shape
    half = d // 2
    beam_stride = device_count // BEAMS
    own_expert = device_index // SPLIT
    bf16 = jnp.bfloat16
    f32 = jnp.float32
    middle = experts // 2

    other = [swapped(w_gate, CORE), swapped(w_up, CORE)]
    carried = tailed(hidden_rows, parents.reshape(rows), lengths)
    planes = [carried] + [swapped(carried, SPLIT * k) for k in range(1, experts)]
    own_a = stacked(planes[:middle])
    x_a, y_a = swapped(own_a, X), swapped(own_a, Y)
    x_a, y_a, planes[2], planes[3], w_down_out, *other[:2] = tied(x_a, y_a, planes[2], planes[3], w_down, *other[:2])
    other.append(swapped(w_down_out, CORE))
    rows_a = [own_a, x_a, y_a, swapped(x_a[:, :half], Y), swapped(y_a[:, half:d], X)]
    own_b = stacked(planes[middle:])
    x_b, y_b = swapped(own_b, X), swapped(own_b, Y)
    packets, facts = packing_call([own_a, y_a, own_b, y_b], latent_cache)
    rows_b = [own_b, x_b, y_b, swapped(x_b[:, :half], Y), swapped(y_b[:, half:d], X)]
    groups = [[b * beam_stride + r for b in range(BEAMS)] for r in range(beam_stride)]
    arrived = lax.all_to_all(
        packets, "ep", split_axis=0, concat_axis=0, axis_index_groups=groups, tiled=True
    )

    near_a, far_a, near_b, far_b = expert_outputs(rows_a, rows_b, [w_gate, w_up, w_down] + other)


    def joined(near, far):
        quad = far.shape[0]
        got_a, got_b = swapped(far[:, :half], X), swapped(far[:, half:], Y)
        return whole_call(join_kernel, [near, got_a, got_b], [((quad, d), bf16)] * 3)

    def totals(mine, for_x, for_y, count):
        return whole_call(
            total_kernel, [mine, swapped(for_x, X), swapped(for_y, Y)], [((rows, d), bf16)] * count
        )
    mine_b, to_x_b, to_y_b = joined(near_b, far_b)
    sums_b = totals(mine_b, to_x_b, to_y_b, experts - middle)
    mine_a, to_x_a, to_y_a = joined(near_a, far_a)
    sums_a = totals(mine_a, to_x_a, to_y_a, middle)
    moe = None
    for k, piece in enumerate(list(sums_a) + list(sums_b)):
        if k:
            piece = swapped(piece, SPLIT * k)
        weight = jnp.sum(
            jnp.where(expert_ids == (own_expert ^ k), gate_weights, 0.0), axis=1, keepdims=True
        )
        term = weight * piece.astype(f32)
        moe = term if moe is None else moe + term
    moe_out = moe.astype(bf16)
    new_cache = unpacking_call(
        facts,
        own_a.shape[0],
        new_latent.astype(f32)[:, None, :],
        arrived,
        jax.ShapeDtypeStruct(latent_cache.shape, bf16),
    )
    return (moe_out, new_cache)


def local(
    hidden_rows,
    expert_ids,
    gate_weights,
    w_gate,
    w_up,
    w_down,
    latent_cache,
    new_latent,
    parents,
    lengths,
):
    device_count = lax.axis_size("ep")
    device_index = lax.axis_index("ep")
    beam_stride = device_count // BEAMS
    own_beam = device_index // beam_stride
    request_block = device_index % beam_stride
    local_rows = hidden_rows.shape[0]
    experts = device_count // SPLIT
    capacity = max(2, min(local_rows, (2 * local_rows * TOP + experts - 1) // experts))
    if capacity == local_rows and experts & (experts - 1) == 0 and beam_stride * 2 == SPLIT:
        return dense_local(
            hidden_rows,
            expert_ids,
            gate_weights,
            w_gate,
            w_up,
            w_down,
            latent_cache,
            new_latent,
            parents,
            lengths,
        )
    expert_range = jnp.arange(experts, dtype=jnp.int32)
    chosen = expert_ids[:, :, None] == expert_range[None, None, :]
    hit_count = jnp.sum(chosen.astype(jnp.int32), axis=1)
    before = jnp.cumsum(hit_count, axis=0) - hit_count
    position = jnp.sum(jnp.where(chosen, before[:, None, :], 0), axis=2)
    slot_range = jnp.arange(capacity, dtype=jnp.int32)
    placer = (hit_count.T[:, None, :] == 1) & (before.T[:, None, :] == slot_range[None, :, None])
    outgoing = jnp.einsum(
        "ecr,rd->ecd", placer.astype(jnp.bfloat16), hidden_rows, preferred_element_type=jnp.float32
    ).astype(jnp.bfloat16)
    copies = jnp.broadcast_to(outgoing[:, None], (experts, SPLIT, capacity, D)).reshape(
        device_count, capacity, D
    )
    received = lax.all_to_all(copies, "ep", split_axis=0, concat_axis=0, tiled=True)
    item_count = received.shape[1]
    flat_rows = received.reshape(device_count * item_count, D)
    gate_proj = jnp.dot(flat_rows, w_gate, preferred_element_type=jnp.float32)
    up_proj = jnp.dot(flat_rows, w_up, preferred_element_type=jnp.float32)
    activated = (jax.nn.silu(gate_proj) * up_proj).astype(jnp.bfloat16)
    partial_value = jnp.dot(activated, w_down, preferred_element_type=jnp.float32).astype(
        jnp.bfloat16
    )
    partial_value = partial_value.reshape(device_count, item_count, D)
    result = lax.all_to_all(partial_value, "ep", split_axis=0, concat_axis=0, tiled=True)
    all_parents, all_lengths = (
        lax.all_gather(parents[:, 0], "ep", axis=0, tiled=True),
        lax.all_gather(lengths, "ep", axis=0, tiled=True),
    )
    parent_grid = lax.dynamic_index_in_dim(
        all_parents.reshape(BEAMS, beam_stride, local_rows), request_block, 1, keepdims=False
    )
    length_grid = lax.dynamic_index_in_dim(
        all_lengths.reshape(BEAMS, beam_stride, local_rows), request_block, 1, keepdims=False
    )
    cache_flat = latent_cache.reshape(local_rows, latent_cache.shape[1] * latent_cache.shape[2])
    packet_range = jnp.arange(CAP, dtype=jnp.int32)

    def selector(target_beam, source_beam):
        wanted = jnp.take(parent_grid, target_beam, axis=0) == source_beam
        ranked = jnp.cumsum(wanted.astype(jnp.int32)) - 1
        return ((ranked[None, :] == packet_range[:, None]) & wanted[None, :]).astype(jnp.bfloat16)

    def packet(target_beam):
        return jnp.dot(
            selector(target_beam, own_beam), cache_flat, preferred_element_type=jnp.float32
        ).astype(jnp.bfloat16)

    arrived = [packet(own_beam)]
    sources = [own_beam]
    for offset in range(1, BEAMS):
        arrived.append(
            passed_along(packet((own_beam + offset) % BEAMS), "ep", offset * beam_stride)
        )
        sources.append((own_beam - offset) % BEAMS)
    stacked = jnp.stack(arrived)
    pickers = jnp.stack([selector(own_beam, source_beam) for source_beam in sources])
    migrated = jnp.einsum(
        "acr,acf->rf", pickers, stacked, preferred_element_type=jnp.float32
    ).reshape(latent_cache.shape)
    own_parents = jnp.take(parent_grid, own_beam, axis=0)
    parent_len = jnp.sum(
        jnp.where(
            jnp.arange(BEAMS, dtype=jnp.int32)[:, None] == own_parents[None, :], length_grid, 0
        ),
        axis=0,
    )
    token_place = jnp.arange(latent_cache.shape[1], dtype=jnp.int32)[None, :, None]
    parent_bound = parent_len[:, None, None]
    appended = new_latent.astype(jnp.float32)[:, None, :]
    new_cache = jnp.where(
        token_place < parent_bound, migrated, jnp.where(token_place == parent_bound, appended, 0.0)
    ).astype(jnp.bfloat16)
    grouped = result.reshape(experts, SPLIT, capacity, D)
    expert_out = jnp.sum(grouped.astype(jnp.float32), axis=1).astype(jnp.bfloat16)
    flat_out = expert_out.reshape(experts * capacity, D)
    picked = flat_out[expert_ids * capacity + position]
    moe_out = jnp.sum(gate_weights[:, :, None] * picked.astype(jnp.float32), axis=1).astype(
        jnp.bfloat16
    )
    return (moe_out, new_cache)


def solution(mesh):
    placed = (
        P(("groups", "ep"), None),
        P(("groups", "ep"), None),
        P(("groups", "ep"), None),
        P(None, "ep"),
        P(None, "ep"),
        P("ep", None),
        P(("groups", "ep"), None, None),
        P(("groups", "ep"), None),
        P(("groups", "ep"), None),
        P(("groups", "ep")),
    )
    return jax.shard_map(
        local,
        mesh=mesh,
        in_specs=placed,
        out_specs=(P(("groups", "ep"), None), P(("groups", "ep"), None, None)),
        check_vma=False,
    )
```

```python
import jax
import jax.numpy as jnp
from jax import lax
from jax.experimental import pallas as pl
from jax.experimental.pallas import tpu as pltpu
from jax.sharding import PartitionSpec as P

D = 7168
TOP = 2
BEAMS = 8
SPLIT = 8
CAP = 2
CORE, X, Y = 1, 2, 4
LANES = 128
STEPS = 4
MIB = 1024 * 1024


def passed_along(value, axis, by):
    peers = lax.axis_size(axis)
    return lax.ppermute(value, axis, [(i, (i + by) % peers) for i in range(peers)])


def swapped(value, mask):
    peers = lax.axis_size("ep")
    return lax.ppermute(value, "ep", [(i, i ^ mask) for i in range(peers)])


def dot32(a, b):
    return jnp.dot(a, b, preferred_element_type=jnp.float32)


def in_vmem(value):
    return pltpu.with_memory_space_constraint(value, pltpu.VMEM)


def in_hbm(value):
    return pltpu.with_memory_space_constraint(value, pltpu.HBM)


def whole_call(body, ins, outs, limit=4, scratch=(), flops=0):
    whole = pl.BlockSpec(memory_space=pltpu.VMEM)
    far = pl.BlockSpec(memory_space=pltpu.HBM)
    arrays = [a[0] if isinstance(a, tuple) else a for a in ins]
    moved = sum(a.size * a.dtype.itemsize for a in arrays)
    return pl.pallas_call(
        body,
        in_specs=[far if isinstance(a, tuple) else whole for a in ins],
        out_specs=[whole] * len(outs),
        out_shape=[pltpu.VMEM(shape, dtype) for shape, dtype in outs],
        scratch_shapes=list(scratch),
        compiler_params=pltpu.CompilerParams(vmem_limit_bytes=limit * MIB),
        cost_estimate=pl.CostEstimate(flops=flops, bytes_accessed=moved, transcendentals=0),
    )(*[in_hbm(a[0]) if isinstance(a, tuple) else in_vmem(a) for a in ins])


def tailed_kernel(parents, lengths, rows, out, parent, length, sems):
    d = rows.shape[1]
    copies = [
        pltpu.make_async_copy(parents, parent, sems.at[0]),
        pltpu.make_async_copy(lengths, length, sems.at[1]),
        pltpu.make_async_copy(rows, out.at[:, pl.ds(0, d)], sems.at[2]),
    ]
    for copy in copies:
        copy.start()
    shape = (rows.shape[0], LANES)
    row = lax.broadcasted_iota(jnp.int32, shape, 0)
    lane = lax.broadcasted_iota(jnp.int32, shape, 1)
    tail = jnp.zeros(shape, jnp.int32)
    copies[0].wait()
    copies[1].wait()
    for i in range(shape[0]):
        tail = jnp.where((row == i) & (lane == 0), parent[i], tail)
        tail = jnp.where((row == i) & (lane == 1), length[i], tail)
    out[:, d:] = tail.astype(jnp.float32).astype(out.dtype)
    copies[2].wait()


def tailed(rows, parents, lengths):
    count, d = rows.shape
    return pl.pallas_call(
        tailed_kernel,
        in_specs=[pl.BlockSpec(memory_space=pltpu.HBM)] * 3,
        out_specs=pl.BlockSpec(memory_space=pltpu.VMEM),
        out_shape=pltpu.VMEM((count, d + LANES), rows.dtype),
        scratch_shapes=[
            pltpu.SMEM((count,), jnp.int32),
            pltpu.SMEM((count,), jnp.int32),
            pltpu.SemaphoreType.DMA((3,)),
        ],
        compiler_params=pltpu.CompilerParams(vmem_limit_bytes=2 * MIB),
        cost_estimate=pl.CostEstimate(flops=0, bytes_accessed=4 * count * d, transcendentals=0),
    )(in_hbm(parents), in_hbm(lengths), in_hbm(rows))


def stack_kernel(*refs):
    ins, out = refs[:-1], refs[-1]
    out[...] = jnp.concatenate([r[...].astype(jnp.float32) for r in ins], axis=0).astype(out.dtype)


def stacked(pieces):
    rows = sum(p.shape[0] for p in pieces)
    return whole_call(stack_kernel, pieces, [((rows, pieces[0].shape[1]), pieces[0].dtype)])[0]


def expert_kernel(*refs):
    groups, sources, outs = (refs[:5], refs[5:10]), refs[10:16], refs[16:20]
    held, (gate_sum, up_sum, act, sems) = refs[20:26], refs[26:]
    d, hid = held[0].shape
    chunk = d // STEPS
    half = d // 2
    quad = groups[0][0].shape[0]
    cuts = [slice(step * chunk, (step + 1) * chunk) for step in range(STEPS)]
    copies = {}
    for step, cut in enumerate(cuts):
        for at in (0, 1, 3, 4):
            copies[at, step] = pltpu.make_async_copy(
                sources[at].at[cut, :], held[at].at[cut, :], sems.at[at, step]
            )
    for step, cut in enumerate(cuts):
        for at in (2, 5):
            copies[at, step] = pltpu.make_async_copy(
                sources[at].at[:, cut], held[at].at[:, cut], sems.at[at, step]
            )
    for copy in copies.values():
        copy.start()
    for step, cut in enumerate(cuts):
        blocks = []
        for own, from_x, from_y, left, right in groups:
            corner = left[:, cut] if cut.stop <= half else right[:, cut.start - half : cut.stop - half]
            blocks += [own[:, cut], from_x[:, cut], from_y[:, cut], corner]
        block = jnp.concatenate(blocks, axis=0)
        for core in range(2):
            units = slice(core * hid, (core + 1) * hid)
            copies[3 * core, step].wait()
            gate = dot32(block, held[3 * core][cut, :])
            copies[3 * core + 1, step].wait()
            up = dot32(block, held[3 * core + 1][cut, :])
            if step:
                gate, up = gate_sum[:, units] + gate, up_sum[:, units] + up
            if step < STEPS - 1:
                gate_sum[:, units] = gate
                up_sum[:, units] = up
            else:
                act[:, units] = (gate / (1.0 + jnp.exp(-gate)) * up).astype(act.dtype)
    for step, cut in enumerate(cuts):
        for at in (2, 5):
            copies[at, step].wait()
        part = (dot32(act[:, :hid], held[2][:, cut]) + dot32(act[:, hid:], held[5][:, cut])).astype(outs[0].dtype)
        for i in range(2):
            start = 4 * quad * i
            outs[2 * i][:, cut] = part[start : start + 3 * quad]
            outs[2 * i + 1][:, cut] = part[start + 3 * quad : start + 4 * quad]


def expert_outputs(rows_a, rows_b, weights):
    quad = rows_a[0].shape[0]
    d, hid = weights[0].shape
    bf16, f32 = jnp.bfloat16, jnp.float32
    outs = [((3 * quad, d), bf16), ((quad, d), bf16)] * 2
    scratch = [pltpu.VMEM(w.shape, w.dtype) for w in weights] + [
        pltpu.VMEM((8 * quad, 2 * hid), f32),
        pltpu.VMEM((8 * quad, 2 * hid), f32),
        pltpu.VMEM((8 * quad, 2 * hid), bf16),
        pltpu.SemaphoreType.DMA((6, STEPS)),
    ]
    flops = 2 * 8 * quad * d * 2 * hid * 3
    return whole_call(expert_kernel, rows_a + rows_b + [(w,) for w in weights], outs, 32, scratch, flops)


def join_kernel(near, got_a, got_b, mine, for_x, for_y):
    f32 = jnp.float32
    q = mine.shape[0]
    half = got_a.shape[1]
    mine[...] = near[:q, :]
    for_x[:, :half] = near[q : 2 * q, :half]
    for_x[:, half:] = (near[q : 2 * q, half:].astype(f32) + got_b[...].astype(f32)).astype(for_x.dtype)
    for_y[:, :half] = (near[2 * q :, :half].astype(f32) + got_a[...].astype(f32)).astype(for_y.dtype)
    for_y[:, half:] = near[2 * q :, half:]


def total_kernel(mine, back_x, back_y, *outs):
    f32 = jnp.float32
    total = mine[...].astype(f32) + back_x[...].astype(f32) + back_y[...].astype(f32)
    rows = outs[0].shape[0]
    for i, out in enumerate(outs):
        out[...] = total[i * rows : (i + 1) * rows].astype(out.dtype)


def read_facts(pieces, facts, scalars, sem):
    quad = pieces[0].shape[0]
    d = pieces[0].shape[1] - LANES
    for i, piece in enumerate(pieces):
        facts[i * quad : (i + 1) * quad, :] = piece[:, d:].astype(jnp.float32).astype(jnp.int32)
    copy = pltpu.make_async_copy(facts, scalars, sem)
    copy.start()
    copy.wait()


def fact_row(place, quad, rows):
    planes = quad // rows
    plane, side = place // 2, place % 2
    return ((plane // planes) * 2 + side) * quad + (plane % planes) * rows


def own_beam():
    return lax.div(lax.axis_index("ep"), lax.axis_size("ep") // BEAMS)


def packing_kernel(own_a, y_a, own_b, y_b, cache, out, facts, scalars, held, sem, cache_sem):
    fetch = pltpu.make_async_copy(cache, held, cache_sem)
    fetch.start()
    read_facts([own_a, y_a, own_b, y_b], facts, scalars, sem)
    rows = cache.shape[0]
    beam = own_beam()
    fetch.wait()
    for place in range(BEAMS):
        at = fact_row(place, own_a.shape[0], rows)
        first = second = count = jnp.int32(0)
        for row in range(rows):
            hit = scalars[at + row, 0] == beam
            first = jnp.where(hit & (count == 0), row, first)
            second = jnp.where(hit & (count == 1), row, second)
            count = count + hit.astype(jnp.int32)
        pair = [held[pick].astype(jnp.float32) for pick in (first, second)]
        out[beam ^ place] = jnp.concatenate(pair, axis=1).astype(out.dtype)


def unpacking_kernel(quad, facts, newest, arrived, out, scalars, sem):
    copy = pltpu.make_async_copy(facts, scalars, sem)
    copy.start()
    copy.wait()
    rows, tokens, width = out.shape
    planes = quad // rows
    beam = own_beam()
    for row in range(rows):
        parent = scalars[row, 0]
        rank = sum([(scalars[other, 0] == parent).astype(jnp.int32) for other in range(row)], jnp.int32(0))
        place = parent ^ beam
        plane, side = place // 2, place % 2
        at = ((plane // planes) * 2 + side) * quad + (plane % planes) * rows + row
        bound = scalars[at, 1]
        token = lax.broadcasted_iota(jnp.int32, (tokens, width), 0)
        pair = arrived[parent].astype(jnp.float32)
        old = jnp.where(rank == 0, pair[:, :width], pair[:, width:])
        value = jnp.where(token < bound, old, jnp.where(token == bound, newest[row], 0.0))
        out[row] = value.astype(out.dtype)


def packing_call(blocks, cache):
    whole = pl.BlockSpec(memory_space=pltpu.VMEM)
    table = (len(blocks) * blocks[0].shape[0], LANES)
    return pl.pallas_call(
        packing_kernel,
        in_specs=[whole] * len(blocks) + [pl.BlockSpec(memory_space=pltpu.HBM)],
        out_specs=[whole] * 2,
        out_shape=[
            jax.ShapeDtypeStruct((BEAMS, cache.shape[1], CAP * cache.shape[2]), cache.dtype),
            pltpu.VMEM(table, jnp.int32),
        ],
        scratch_shapes=[
            pltpu.SMEM(table, jnp.int32),
            pltpu.VMEM(cache.shape, cache.dtype),
            pltpu.SemaphoreType.DMA,
            pltpu.SemaphoreType.DMA,
        ],
        compiler_params=pltpu.CompilerParams(vmem_limit_bytes=4 * MIB),
        cost_estimate=pl.CostEstimate(flops=0, bytes_accessed=4 * cache.size, transcendentals=0),
    )(*[in_vmem(b) for b in blocks], in_hbm(cache))


def unpacking_call(facts, quad, newest, arrived, shape):
    whole = pl.BlockSpec(memory_space=pltpu.VMEM)
    return pl.pallas_call(
        lambda *refs: unpacking_kernel(quad, *refs),
        in_specs=[whole] * 3,
        out_specs=whole,
        out_shape=shape,
        scratch_shapes=[pltpu.SMEM(facts.shape, jnp.int32), pltpu.SemaphoreType.DMA],
        compiler_params=pltpu.CompilerParams(vmem_limit_bytes=6 * MIB),
        cost_estimate=pl.CostEstimate(
            flops=0, bytes_accessed=4 * newest.size * shape.shape[1], transcendentals=0
        ),
    )(facts, newest, arrived)


def tied(*values):
    return lax.optimization_barrier(values)


def dense_local(
    hidden_rows,
    expert_ids,
    gate_weights,
    w_gate,
    w_up,
    w_down,
    latent_cache,
    new_latent,
    parents,
    lengths,
):
    device_count = lax.axis_size("ep")
    device_index = lax.axis_index("ep")
    experts = device_count // SPLIT
    rows, d = hidden_rows.shape
    half = d // 2
    beam_stride = device_count // BEAMS
    own_expert = device_index // SPLIT
    bf16 = jnp.bfloat16
    f32 = jnp.float32
    middle = experts // 2

    other = [swapped(w_gate, CORE), swapped(w_up, CORE)]
    carried = tailed(hidden_rows, parents.reshape(rows), lengths)
    planes = [carried] + [swapped(carried, SPLIT * k) for k in range(1, experts)]
    own_a = stacked(planes[:middle])
    x_a, y_a = swapped(own_a, X), swapped(own_a, Y)
    x_a, y_a, planes[2], planes[3], w_down_out, *other[:2] = tied(x_a, y_a, planes[2], planes[3], w_down, *other[:2])
    other.append(swapped(w_down_out, CORE))
    rows_a = [own_a, x_a, y_a, swapped(x_a[:, :half], Y), swapped(y_a[:, half:d], X)]
    own_b = stacked(planes[middle:])
    x_b, y_b = swapped(own_b, X), swapped(own_b, Y)
    packets, facts = packing_call([own_a, y_a, own_b, y_b], latent_cache)
    rows_b = [own_b, x_b, y_b, swapped(x_b[:, :half], Y), swapped(y_b[:, half:d], X)]
    groups = [[b * beam_stride + r for b in range(BEAMS)] for r in range(beam_stride)]
    arrived = lax.all_to_all(
        packets, "ep", split_axis=0, concat_axis=0, axis_index_groups=groups, tiled=True
    )

    near_a, far_a, near_b, far_b = expert_outputs(rows_a, rows_b, [w_gate, w_up, w_down] + other)


    def joined(near, far):
        quad = far.shape[0]
        got_a, got_b = swapped(far[:, :half], X), swapped(far[:, half:], Y)
        return whole_call(join_kernel, [near, got_a, got_b], [((quad, d), bf16)] * 3)

    def totals(mine, for_x, for_y, count):
        return whole_call(
            total_kernel, [mine, swapped(for_x, X), swapped(for_y, Y)], [((rows, d), bf16)] * count
        )
    mine_b, to_x_b, to_y_b = joined(near_b, far_b)
    sums_b = totals(mine_b, to_x_b, to_y_b, experts - middle)
    mine_a, to_x_a, to_y_a = joined(near_a, far_a)
    sums_a = totals(mine_a, to_x_a, to_y_a, middle)
    moe = None
    for k, piece in enumerate(list(sums_a) + list(sums_b)):
        if k:
            piece = swapped(piece, SPLIT * k)
        weight = jnp.sum(
            jnp.where(expert_ids == (own_expert ^ k), gate_weights, 0.0), axis=1, keepdims=True
        )
        term = weight * piece.astype(f32)
        moe = term if moe is None else moe + term
    moe_out = moe.astype(bf16)
    new_cache = unpacking_call(
        facts,
        own_a.shape[0],
        new_latent.astype(f32)[:, None, :],
        arrived,
        jax.ShapeDtypeStruct(latent_cache.shape, bf16),
    )
    return (moe_out, new_cache)


def local(
    hidden_rows,
    expert_ids,
    gate_weights,
    w_gate,
    w_up,
    w_down,
    latent_cache,
    new_latent,
    parents,
    lengths,
):
    device_count = lax.axis_size("ep")
    device_index = lax.axis_index("ep")
    beam_stride = device_count // BEAMS
    own_beam = device_index // beam_stride
    request_block = device_index % beam_stride
    local_rows = hidden_rows.shape[0]
    experts = device_count // SPLIT
    capacity = max(2, min(local_rows, (2 * local_rows * TOP + experts - 1) // experts))
    if capacity == local_rows and experts & (experts - 1) == 0 and beam_stride * 2 == SPLIT:
        return dense_local(
            hidden_rows,
            expert_ids,
            gate_weights,
            w_gate,
            w_up,
            w_down,
            latent_cache,
            new_latent,
            parents,
            lengths,
        )
    expert_range = jnp.arange(experts, dtype=jnp.int32)
    chosen = expert_ids[:, :, None] == expert_range[None, None, :]
    hit_count = jnp.sum(chosen.astype(jnp.int32), axis=1)
    before = jnp.cumsum(hit_count, axis=0) - hit_count
    position = jnp.sum(jnp.where(chosen, before[:, None, :], 0), axis=2)
    slot_range = jnp.arange(capacity, dtype=jnp.int32)
    placer = (hit_count.T[:, None, :] == 1) & (before.T[:, None, :] == slot_range[None, :, None])
    outgoing = jnp.einsum(
        "ecr,rd->ecd", placer.astype(jnp.bfloat16), hidden_rows, preferred_element_type=jnp.float32
    ).astype(jnp.bfloat16)
    copies = jnp.broadcast_to(outgoing[:, None], (experts, SPLIT, capacity, D)).reshape(
        device_count, capacity, D
    )
    received = lax.all_to_all(copies, "ep", split_axis=0, concat_axis=0, tiled=True)
    item_count = received.shape[1]
    flat_rows = received.reshape(device_count * item_count, D)
    gate_proj = jnp.dot(flat_rows, w_gate, preferred_element_type=jnp.float32)
    up_proj = jnp.dot(flat_rows, w_up, preferred_element_type=jnp.float32)
    activated = (jax.nn.silu(gate_proj) * up_proj).astype(jnp.bfloat16)
    partial_value = jnp.dot(activated, w_down, preferred_element_type=jnp.float32).astype(
        jnp.bfloat16
    )
    partial_value = partial_value.reshape(device_count, item_count, D)
    result = lax.all_to_all(partial_value, "ep", split_axis=0, concat_axis=0, tiled=True)
    all_parents, all_lengths = (
        lax.all_gather(parents[:, 0], "ep", axis=0, tiled=True),
        lax.all_gather(lengths, "ep", axis=0, tiled=True),
    )
    parent_grid = lax.dynamic_index_in_dim(
        all_parents.reshape(BEAMS, beam_stride, local_rows), request_block, 1, keepdims=False
    )
    length_grid = lax.dynamic_index_in_dim(
        all_lengths.reshape(BEAMS, beam_stride, local_rows), request_block, 1, keepdims=False
    )
    cache_flat = latent_cache.reshape(local_rows, latent_cache.shape[1] * latent_cache.shape[2])
    packet_range = jnp.arange(CAP, dtype=jnp.int32)

    def selector(target_beam, source_beam):
        wanted = jnp.take(parent_grid, target_beam, axis=0) == source_beam
        ranked = jnp.cumsum(wanted.astype(jnp.int32)) - 1
        return ((ranked[None, :] == packet_range[:, None]) & wanted[None, :]).astype(jnp.bfloat16)

    def packet(target_beam):
        return jnp.dot(
            selector(target_beam, own_beam), cache_flat, preferred_element_type=jnp.float32
        ).astype(jnp.bfloat16)

    arrived = [packet(own_beam)]
    sources = [own_beam]
    for offset in range(1, BEAMS):
        arrived.append(
            passed_along(packet((own_beam + offset) % BEAMS), "ep", offset * beam_stride)
        )
        sources.append((own_beam - offset) % BEAMS)
    stacked = jnp.stack(arrived)
    pickers = jnp.stack([selector(own_beam, source_beam) for source_beam in sources])
    migrated = jnp.einsum(
        "acr,acf->rf", pickers, stacked, preferred_element_type=jnp.float32
    ).reshape(latent_cache.shape)
    own_parents = jnp.take(parent_grid, own_beam, axis=0)
    parent_len = jnp.sum(
        jnp.where(
            jnp.arange(BEAMS, dtype=jnp.int32)[:, None] == own_parents[None, :], length_grid, 0
        ),
        axis=0,
    )
    token_place = jnp.arange(latent_cache.shape[1], dtype=jnp.int32)[None, :, None]
    parent_bound = parent_len[:, None, None]
    appended = new_latent.astype(jnp.float32)[:, None, :]
    new_cache = jnp.where(
        token_place < parent_bound, migrated, jnp.where(token_place == parent_bound, appended, 0.0)
    ).astype(jnp.bfloat16)
    grouped = result.reshape(experts, SPLIT, capacity, D)
    expert_out = jnp.sum(grouped.astype(jnp.float32), axis=1).astype(jnp.bfloat16)
    flat_out = expert_out.reshape(experts * capacity, D)
    picked = flat_out[expert_ids * capacity + position]
    moe_out = jnp.sum(gate_weights[:, :, None] * picked.astype(jnp.float32), axis=1).astype(
        jnp.bfloat16
    )
    return (moe_out, new_cache)


def solution(mesh):
    placed = (
        P(("groups", "ep"), None),
        P(("groups", "ep"), None),
        P(("groups", "ep"), None),
        P(None, "ep"),
        P(None, "ep"),
        P("ep", None),
        P(("groups", "ep"), None, None),
        P(("groups", "ep"), None),
        P(("groups", "ep"), None),
        P(("groups", "ep")),
    )
    return jax.shard_map(
        local,
        mesh=mesh,
        in_specs=placed,
        out_specs=(P(("groups", "ep"), None), P(("groups", "ep"), None, None)),
        check_vma=False,
    )
```
